256 devices in a mesh: row: 16 (over x_lo, z), col: 16 (over y, x_hi, core).
Axes of the slice: x: 4 (x_hi: 2, x_lo: 2; x = x_hi * 2 + x_lo), y: 4, z: 8, core: 2. Of those that a mesh axis runs over, the one named last changes fastest.
Arguments:
- features: bfloat16 [131072, 256], P(('row', 'col')), may hold values from -6 to 6
- tiles: int32 [16, 16, 96, 128, 128], P('row', 'col'), may hold values from 0 to 2
- tile_rows: int32 [16, 16, 96], P('row', 'col'), may hold values from 0 to 63
- tile_cols: int32 [16, 16, 96], P('row', 'col'), may hold values from 0 to 31, as said below
- tile_count: int32 [16, 16], P('row', 'col'), may hold values from 1 to 96, as said below
- panel_lists: int32 [16, 16, 16, 2], P('row', 'col'), may hold values from -1 to 3, as said below
- self_weight: bfloat16 [256, 256], replicated, may hold values from -0.375 to 0.375
- neigh_weight: bfloat16 [256, 256], replicated, may hold values from -6 to 6
- bias: float32 [256], replicated, may hold values from -3 to 3
Outputs:
- hidden: bfloat16 [131072, 256], P(('row', 'col'))
The draws below stay inside these ranges and needn't reach their ends.
Inputs may be any that keep to these rules, and one draw needn't show every extreme that they name: `panel_lists`: every live tile names a non-empty list entry; each device reads exactly 2 distinct panels from at least one owner and 1 to 2 from every owner; empty entries come last in a list. `tile_cols`: every entry names a non-empty slot of the device's list. `tile_count`: some device holds 96 live tiles.
All inputs are finite; a program needn't handle non-finite values.
Results may differ from the reference program's by a relative error of at most 0.013.
Values may be sent and summed in bfloat16 or wider, within the bound.
A program may use at most 128 MiB of HBM per device.

```python
import math
import jax
import jax.numpy as jnp
import numpy as np
from jax import lax

FEAT = 256
TILE = 128
PANELS_DEV = 4
TILES = 96
CAP = 2
NODES = 131072
N_ROW = 16
N_COL = 16


def shared_lists(key):
    score_key, count_key, full_key = jax.random.split(key, 3)
    scores = jax.random.randint(score_key, (N_ROW, N_COL, N_ROW, PANELS_DEV), 0, 1 << 20)
    scores = scores * PANELS_DEV + jnp.arange(PANELS_DEV, dtype=jnp.int32)
    order = jnp.argsort(scores, axis=-1, stable=True).astype(jnp.int32)[..., :CAP]
    counts = jax.random.randint(count_key, (N_ROW, N_COL, N_ROW), 1, CAP + 1)
    full_owner = jax.random.randint(full_key, (N_ROW, N_COL, 1), 0, N_ROW)
    counts = jnp.where(jnp.arange(N_ROW, dtype=jnp.int32) == full_owner, CAP, counts)
    slot_ids = jnp.arange(CAP, dtype=jnp.int32)
    wanted = jnp.where(slot_ids < counts[..., None], order, -1)
    return (wanted, counts)


def draw_panel_lists(key, part):
    wanted, counts = shared_lists(key)
    return wanted.astype(jnp.int32)


def draw_tile_cols(key, part):
    wanted, counts = shared_lists(key)
    key = jax.random.fold_in(key, 7)
    owner_key, slot_key = jax.random.split(key)
    owners = jax.random.randint(owner_key, (N_ROW, N_COL, TILES), 0, N_ROW)
    limits = jnp.take_along_axis(counts, owners, axis=2)
    slot_index = jax.random.randint(slot_key, (N_ROW, N_COL, TILES), 0, 1 << 20) % limits
    return (owners * CAP + slot_index).astype(jnp.int32)


def draw_tile_count(key, part):
    key = jax.random.fold_in(key, 11)
    count_key, full_key = jax.random.split(key)
    counts = jax.random.randint(count_key, (N_ROW * N_COL,), max(TILES // 4, 1), TILES + 1)
    full_device = jax.random.randint(full_key, (), 0, N_ROW * N_COL)
    counts = jnp.where(jnp.arange(N_ROW * N_COL, dtype=jnp.int32) == full_device, TILES, counts)
    return counts.reshape(N_ROW, N_COL).astype(jnp.int32)


def touch_ends(result, stream_key, low, high):
    place = [jax.random.randint(jax.random.fold_in(stream_key, axis), (), 0, length) for axis, length in enumerate(result.shape)]
    longest = result.shape.index(max(result.shape))
    beside = place[:longest] + [(place[longest] + 1) % result.shape[longest]] + place[longest + 1:]
    return result.at[tuple(place)].set(low).at[tuple(beside)].set(high)


def block_levels(stream_key, extent, shards, smallest, top_value):
    gain, own = 1.0, jax.random.fold_in(stream_key, 6)
    for position, parts in shards:
        draws = jnp.exp(jax.random.uniform(jax.random.fold_in(own, position), (parts,), jnp.float32, smallest / len(shards), top_value / len(shards)))
        gain = gain * jnp.repeat(draws, extent[position] // parts).reshape([-1 if axis == position else 1 for axis in range(len(extent))])
    return gain


def rank_table(count, skew):
    weights = [(1 << 20) // math.isqrt(rank ** skew) + 1 for rank in range(1, count + 1)]
    deviation = 1 + sum(weights) // (1 << 30)
    return np.cumsum(np.array([max(1, weight // deviation) for weight in weights]))


def ranked(stream_key, extent, number_of, skew):
    listing = rank_table(number_of, skew)
    pick = jax.random.randint(jax.random.fold_in(stream_key, 1), extent, 0, int(listing[number_of - 1]))
    grade = jnp.searchsorted(jnp.asarray(listing, jnp.int32), pick, side="right")
    return jax.random.permutation(jax.random.fold_in(stream_key, 2), number_of)[grade].astype(jnp.int32)


def scatter_about(own_key, shape, deviation, limit, pieces=(), kind=jnp.bfloat16):
    result = jax.random.normal(own_key, shape, jnp.float32) * deviation
    if len(pieces) > 0:
        result = block_levels(own_key, shape, pieces, -0.22, 0.18) * result
    return jnp.clip(result, min=-limit, max=limit).astype(kind)


def setup_inputs(seed: int = 0) -> dict:
    key_list = jax.random.split(jax.random.key(seed), 10)
    features = scatter_about(key_list[0], (NODES, FEAT), 1.0, 6.0, ((0, 256),))
    tiles = touch_ends(jax.random.randint(key_list[1], (N_ROW, N_COL, TILES, TILE, TILE), 0, 3), jax.random.fold_in(key_list[1], 1), 0, 2).astype(jnp.int32)
    tile_rows = touch_ends(ranked(key_list[2], (N_ROW, N_COL, TILES), N_COL * PANELS_DEV, 2), jax.random.fold_in(key_list[2], 3), 0, (N_COL * PANELS_DEV) - 1).astype(jnp.int32)
    tile_cols = draw_tile_cols(jax.random.fold_in(key_list[9], 71), 0)
    tile_count = draw_tile_count(jax.random.fold_in(key_list[9], 71), 0)
    panel_lists = draw_panel_lists(jax.random.fold_in(key_list[9], 71), 0)
    self_weight = scatter_about(key_list[6], (FEAT, FEAT), FEAT ** -0.5, 0.375)
    neigh_weight = scatter_about(key_list[7], (FEAT, FEAT), 1 ** -0.5, 6.0)
    bias = scatter_about(key_list[8], (FEAT,), 0.5, 3.0, (), jnp.float32)
    return dict(features=features, tiles=tiles, tile_rows=tile_rows, tile_cols=tile_cols, tile_count=tile_count, panel_lists=panel_lists, self_weight=self_weight, neigh_weight=neigh_weight, bias=bias)


def device_terms(features, tiles, tile_rows, tile_cols, tile_count, panel_lists, block_row, block_col):
    column_panels = features.reshape(N_ROW, N_COL, PANELS_DEV, TILE, FEAT)
    column_block = lax.dynamic_index_in_dim(column_panels, block_col, axis=1, keepdims=False)
    column_block = column_block.reshape(N_ROW * PANELS_DEV, TILE, FEAT)
    wanted_lists = panel_lists[block_row, block_col]
    entries = tile_cols[block_row, block_col]
    owners = entries // CAP
    slot_index = entries % CAP
    chosen = wanted_lists[owners, slot_index]
    panel_index = (owners * PANELS_DEV + jnp.maximum(chosen, 0)).astype(jnp.int32)
    operand = column_block[panel_index].astype(jnp.float32)
    live_tiles = jnp.arange(TILES, dtype=jnp.int32) < tile_count[block_row, block_col]
    blocks = jnp.where(live_tiles[:, None, None], tiles[block_row, block_col], 0)
    products = jnp.einsum("tab,tbf->taf", blocks.astype(jnp.float32), operand)
    row_index = tile_rows[block_row, block_col]
    partial_value = jnp.zeros((N_COL * PANELS_DEV, TILE, FEAT), jnp.float32).at[row_index].add(products)
    counts = jnp.zeros((N_COL * PANELS_DEV, TILE), jnp.float32).at[row_index].add(jnp.sum(blocks, axis=2).astype(jnp.float32))
    rounded = lax.optimization_barrier(partial_value.astype(jnp.bfloat16))
    return rounded.astype(jnp.float32), counts


def reference(features, tiles, tile_rows, tile_cols, tile_count, panel_lists, self_weight, neigh_weight, bias):
    block_nodes = N_COL * PANELS_DEV * TILE

    def one_row(block_row):
        def add_device(step_col, carry):
            block_col = jnp.asarray(step_col).astype(jnp.int32)
            partial_value, counts = device_terms(features, tiles, tile_rows, tile_cols, tile_count, panel_lists, block_row, block_col)
            return (carry[0] + partial_value, carry[1] + counts)

        start = (jnp.zeros((N_COL * PANELS_DEV, TILE, FEAT), jnp.float32), jnp.zeros((N_COL * PANELS_DEV, TILE), jnp.float32))
        summed, degree = lax.fori_loop(0, N_COL, add_device, start)
        mean_rows = (summed / jnp.maximum(degree, 1.0)[:, :, None]).astype(jnp.bfloat16).reshape(block_nodes, FEAT)
        own_rows = lax.dynamic_slice_in_dim(features, (block_row * block_nodes).astype(jnp.int32), block_nodes, 0)
        mixed = jnp.dot(own_rows, self_weight, preferred_element_type=jnp.float32)
        mixed = mixed + jnp.dot(mean_rows, neigh_weight, preferred_element_type=jnp.float32) + bias
        return jnp.maximum(mixed, 0.0).astype(jnp.bfloat16)

    stacked = lax.map(one_row, jnp.arange(N_ROW, dtype=jnp.int32))
    return stacked.reshape(NODES, FEAT)
```

```python
import functools

import jax
import jax.numpy as jnp
from jax import lax
from jax.experimental import pallas as pl
from jax.experimental.pallas import tpu as pltpu
from jax.sharding import PartitionSpec as P

MESH = pl.DeviceIdType.MESH
Z = 8
Y = 4
TILE = 128
HALVES = 2
PANELS = 4
TILES = 96
CAP = 2
COLS = 16
ROWS = 16
CHUNKS = 4
YFIRST = (4, 2)

F32 = jnp.float32
BF16 = jnp.bfloat16


class Sems:
    def __init__(self, send, recv):
        self.send, self.recv, self.used, self.copies = send, recv, 0, []

    def copy(self, src, dst, device):
        n = self.used
        self.used += 1
        c = pltpu.make_async_remote_copy(
            src_ref=src,
            dst_ref=dst,
            send_sem=self.send.at[n],
            recv_sem=self.recv.at[n],
            device_id=device,
            device_id_type=MESH,
        )
        self.copies.append(c)
        return c


def kernel(
    feat_ref,
    tiles_ref,
    rows_ref,
    cols_ref,
    count_ref,
    lists_ref,
    lists_vec_ref,
    ws_ref,
    wn_ref,
    bias_ref,
    out_ref,
    *scratch,
):
    s = dict(zip(SCRATCH_NAMES, scratch))
    r, c = lax.axis_index("row"), lax.axis_index("col")
    x_lo, z = r // Z, lax.rem(r, Z)
    y, x_hi, core = c // 4, lax.rem(c // 2, 2), lax.rem(c, 2)

    def z_at(d):
        return lax.rem(z + d + Z, Z)

    def at_z(d):
        return (x_lo * Z + z_at(d), c)

    def at_y(d):
        return (r, lax.rem(c + 4 * d, COLS))

    x_pair = ((1 - x_lo) * Z + z, c)
    x_far = (r, c + 2 - 4 * x_hi)
    sibling = (r, c + 1 - 2 * core)

    local = s["local_sem"]
    own_copies = []
    for h in range(HALVES):
        cp = pltpu.make_async_copy(
            feat_ref.at[:, :, pl.ds(h * TILE, TILE)], s["own"].at[h], local.at[h]
        )
        cp.start()
        own_copies.append(cp)
    per = TILES // CHUNKS
    tile_copies = []
    for k in range(CHUNKS):
        part = pl.ds(k * per, per)
        cp = pltpu.make_async_copy(
            tiles_ref.at[part], s["tiles32"].at[part], local.at[HALVES + k]
        )
        cp.start()
        tile_copies.append(cp)
    s["lists_out"][...] = jnp.zeros((8, TILE), jnp.int32)
    s["lists_out"][0:1, 0 : ROWS * CAP] = lists_vec_ref[...]

    barrier = pltpu.get_barrier_semaphore()
    peers = [at_z(1), at_z(-1), x_pair]
    for k in range(1, COLS):
        peers.append((r, lax.rem(c + k, COLS)))
    for peer in peers:
        pl.semaphore_signal(barrier, inc=1, device_id=peer, device_id_type=MESH)
    pl.semaphore_wait(barrier, len(peers))

    sems = Sems(s["send_sem"], s["recv_sem"])
    for cp in own_copies:
        cp.wait()

    fwd = [[s[f"fwd{h}{k}"] for k in range(3)] for h in range(HALVES)]
    bwd = [[s[f"bwd{h}{k}"] for k in range(3)] for h in range(HALVES)]
    opp = [s["opp0"], s["opp1"]]
    oper = [s["oper0"], s["oper1"]]
    ring = {}
    for h in range(HALVES):
        for k in range(4):
            if k < 3:
                src_f = s["own"].at[h] if k == 0 else fwd[h][k - 1]
                src_b = s["own"].at[h] if k == 0 else bwd[h][k - 1]
                dst_f, dst_b = fwd[h][k], bwd[h][k]
            else:
                src_f, dst_f = fwd[h][2].at[pl.ds(0, 2)], opp[h].at[pl.ds(0, 2)]
                src_b, dst_b = bwd[h][2].at[pl.ds(2, 2)], opp[h].at[pl.ds(2, 2)]
            ring[h, 0, k] = sems.copy(src_f, dst_f, at_z(1))
            ring[h, 1, k] = sems.copy(src_b, dst_b, at_z(-1))
    lists_copy = sems.copy(s["lists_out"], s["lists_in"], x_pair)

    for h in range(HALVES):
        ring[h, 0, 0].start()
        ring[h, 1, 0].start()
    lists_copy.start()

    pair_copies = {}

    def select(h, slot, block, dist):
        owner = x_lo * Z + z_at(dist)
        for j in range(CAP):
            mine = jnp.maximum(lists_ref[0, owner * CAP + j], 0)
            oper[h][owner * CAP + j] = block[mine]
        for j in range(CAP):
            theirs = jnp.maximum(s["lists_smem"][0, owner * CAP + j], 0)
            s[f"pair{h}"][slot * CAP + j] = block[theirs]
        cp = sems.copy(
            s[f"pair{h}"].at[pl.ds(slot * CAP, CAP)],
            oper[h].at[pl.ds(owner * CAP, CAP)],
            x_pair,
        )
        cp.start()
        pair_copies[h, slot] = cp

    live = count_ref[0, 0]
    lane = lax.broadcasted_iota(jnp.int32, (TILE, TILE), 1)
    sub = lax.broadcasted_iota(jnp.int32, (TILE, TILE), 0)
    s["rows"][...] = jnp.full((8, TILE), -1, jnp.int32)
    s["rows"][0:1, 0:TILES] = rows_ref[...]
    row_l = jnp.broadcast_to(s["rows"][0:1, :], (TILE, TILE))
    row_l = jnp.where(lane < live, row_l, -1)
    row_s = jnp.transpose(row_l.astype(F32)).astype(jnp.int32)
    prev = jnp.max(jnp.where((row_s == row_l) & (sub < lane), sub, -1), axis=0, keepdims=True)
    prev = jnp.where(prev < 0, TILES, prev)
    last = jnp.max(jnp.where(row_s == lane, sub, -1), axis=0, keepdims=True)
    last = jnp.where(last < 0, TILES, last)
    s["meta"][0:1, :] = prev
    s["meta"][1:2, :] = last
    s["meta"][2:8, :] = jnp.zeros((6, TILE), jnp.int32)
    meta_copy = pltpu.make_async_copy(s["meta"], s["meta_smem"], local.at[HALVES + CHUNKS])
    meta_copy.start()

    for h in range(HALVES):
        s[f"sums{h}"][TILES] = jnp.zeros((TILE, TILE), F32)

    lists_copy.wait_recv()
    smem_copy = pltpu.make_async_copy(
        s["lists_in"], s["lists_smem"], local.at[HALVES + CHUNKS + 1]
    )
    smem_copy.start()
    smem_copy.wait()
    for h in range(HALVES):
        select(h, 0, s["own"].at[h], 0)

    ones = jnp.ones((16, TILE), BF16)

    def prepare(k):
        tile_copies[k].wait()

        def body(t, _):
            block = s["tiles32"][t].astype(F32).astype(BF16)
            s["blocks"][t] = block
            sums = lax.dot_general(
                ones, block, (((1,), (1,)), ((), ())), preferred_element_type=F32
            )
            s["degs"][pl.ds(t, 1), :] = sums[0:1, :]
            return 0

        lax.fori_loop(k * per, (k + 1) * per, body, 0, unroll=4)

    def arrive(h, k):
        for way in (0, 1):
            ring[h, way, k].wait_recv()
            if k < 3:
                ring[h, way, k + 1].start()
        if k < 3:
            select(h, 1 + k, fwd[h][k], -(k + 1))
            select(h, 4 + k, bwd[h][k], k + 1)
        else:
            select(h, 7, opp[h], 4)

    def base(i):
        mixed = jnp.dot(s["own"][0, i], ws_ref[0:TILE, :], preferred_element_type=F32)
        mixed += jnp.dot(s["own"][1, i], ws_ref[TILE : 2 * TILE, :], preferred_element_type=F32)
        s["mixed"][i] = mixed + bias_ref[...]

    for k in range(4):
        prepare(k)
        for h in range(HALVES):
            arrive(h, k)
        base(k)

    q = lax.broadcasted_iota(jnp.int32, (TILE, TILE), 0)
    panel = jnp.where(lax.rem(q, 8) < 4, (q // 8) * 4 + lax.rem(q, 8), -2)
    hot = (panel == row_l).astype(F32).astype(BF16)
    s["degs"][TILES:TILE, :] = jnp.zeros((TILE - TILES, TILE), F32)
    degs = jnp.dot(hot, s["degs"][...].astype(BF16), preferred_element_type=F32)
    s["deg_out"][...] = degs.reshape(COLS, 8, TILE)
    deg_copies = []
    for k in range(1, COLS):
        to = lax.rem(c + k, COLS)
        cp = sems.copy(s["deg_out"].at[to], s["deg_in"].at[k - 1], (r, to))
        cp.start()
        deg_copies.append(cp)

    meta_copy.wait()

    def products(h):
        for slot in range(8):
            pair_copies[h, slot].wait_recv()
        sums = s[f"sums{h}"]

        def body(t, _):
            value = jnp.dot(
                s["blocks"][t], oper[h][cols_ref[0, t]], preferred_element_type=F32
            )
            sums[t] = value + sums[s["meta_smem"][0, t]]
            return 0

        lax.fori_loop(0, TILES, body, 0, unroll=4)

    def owner_col(dy, dx, which):
        hi = x_hi if dx == 0 else 1 - x_hi
        return lax.rem(y + dy, Y) * 4 + hi * 2 + which

    order = [(2, 1), (2, 0), (1, 1), (1, 0), (3, 1), (3, 0), (0, 1), (0, 0)]
    swap = {}

    def partial(h, dy, dx, which, i):
        p = owner_col(dy, dx, which) * PANELS + i
        return s[f"sums{h}"][s["meta_smem"][1, p]]

    def exchange(h):
        for dy, dx in order:
            j = dy * 2 + dx

            def body(i, _):
                s["swap_out"][h, j * PANELS + i] = partial(h, dy, dx, 1 - core, i).astype(BF16)
                return 0

            lax.fori_loop(0, PANELS, body, 0, unroll=True)
            part = pl.ds(j * PANELS, PANELS)
            cp = sems.copy(s["swap_out"].at[h, part], s["swap_in"].at[h, part], sibling)
            cp.start()
            swap[h, j] = cp

    def both(h, dy, dx, i):
        j = dy * 2 + dx
        return partial(h, dy, dx, core, i) + s["swap_in"][h, j * PANELS + i].astype(F32)

    stage1, stage2 = {}, {}

    def first(h):
        n = YFIRST[h]
        m = PANELS - n
        arrived = set()

        def need(dy, dx):
            if (dy, dx) not in arrived:
                arrived.add((dy, dx))
                swap[h, dy * 2 + dx].wait_recv()

        for dy in (2, 1, 3):
            need(dy, 1)
            need(dy, 0)
            if n:
                for dx in (1, 0):
                    for i in range(n):
                        s[f"y1_out{h}"][dy - 1, dx * n + i] = both(h, dy, dx, i).astype(BF16)
                cp = sems.copy(
                    s[f"y1_out{h}"].at[dy - 1], s[f"y1_in{h}"].at[dy - 1], at_y(dy)
                )
                cp.start()
                stage1[h, dy] = cp
            if m:
                for i in range(m):
                    s[f"x1_out{h}"][dy, i] = both(h, dy, 1, n + i).astype(BF16)
                cp = sems.copy(s[f"x1_out{h}"].at[dy], s[f"x1_in{h}"].at[dy], x_far)
                cp.start()
                stage1[h, "x", dy] = cp
        need(0, 1)
        need(0, 0)
        if m:
            for i in range(m):
                s[f"x1_out{h}"][0, i] = both(h, 0, 1, n + i).astype(BF16)
            cp = sems.copy(s[f"x1_out{h}"].at[0], s[f"x1_in{h}"].at[0], x_far)
            cp.start()
            stage1[h, "x", 0] = cp

    def second(h):
        n = YFIRST[h]
        m = PANELS - n
        if m:
            for dy in (2, 1, 3):
                stage1[h, "x", dy].wait_recv()
                for i in range(m):
                    total = both(h, dy, 0, n + i) + s[f"x1_in{h}"][dy, i].astype(F32)
                    s[f"y2_out{h}"][dy - 1, i] = total.astype(BF16)
                cp = sems.copy(
                    s[f"y2_out{h}"].at[dy - 1], s[f"y2_in{h}"].at[dy - 1], at_y(dy)
                )
                cp.start()
                stage2[h, dy] = cp
        if n:
            for dy in (2, 1, 3):
                stage1[h, dy].wait_recv()
            for i in range(n):
                total = both(h, 0, 1, i)
                for dy in (2, 1, 3):
                    total += s[f"y1_in{h}"][dy - 1, n + i].astype(F32)
                s[f"x2_out{h}"][i] = total.astype(BF16)
            cp = sems.copy(s[f"x2_out{h}"], s[f"x2_in{h}"], x_far)
            cp.start()
            stage2[h, "x"] = cp

    def third(h):
        n = YFIRST[h]
        m = PANELS - n
        if m:
            stage1[h, "x", 0].wait_recv()
            for dy in (2, 1, 3):
                stage2[h, dy].wait_recv()
        if n:
            stage2[h, "x"].wait_recv()
        for i in range(PANELS):
            total = both(h, 0, 0, i)
            if i < n:
                for dy in (2, 1, 3):
                    total += s[f"y1_in{h}"][dy - 1, i].astype(F32)
                total += s[f"x2_in{h}"][i].astype(F32)
            else:
                total += s[f"x1_in{h}"][0, i - n].astype(F32)
                for dy in (2, 1, 3):
                    total += s[f"y2_in{h}"][dy - 1, i - n].astype(F32)
            mean = (total / s["deg"][i]).astype(BF16)
            s["mixed"][i] += jnp.dot(
                mean, wn_ref[h * TILE : (h + 1) * TILE, :], preferred_element_type=F32
            )

    def degree():
        total = s["deg_out"][c]
        for k in range(1, COLS):
            deg_copies[k - 1].wait_recv()
            total += s["deg_in"][k - 1]
        total = jnp.maximum(total, 1.0)
        wide = jnp.transpose(jnp.concatenate([total] * 16, axis=0))
        for i in range(PANELS):
            s["deg"][i] = jnp.broadcast_to(wide[:, i : i + 1], (TILE, TILE))

    products(0)
    exchange(0)
    degree()
    first(0)
    products(1)
    exchange(1)
    first(1)
    second(0)
    second(1)
    third(0)
    third(1)
    for i in range(PANELS):
        out_ref[pl.ds(i * TILE, TILE), :] = jnp.maximum(s["mixed"][i], 0.0).astype(BF16)
    for cp in sems.copies:
        cp.wait_send()


def scratch_spec():
    panel = lambda *lead: pltpu.VMEM((*lead, TILE, TILE), BF16)
    spec = {
        "send_sem": pltpu.SemaphoreType.DMA((96,)),
        "recv_sem": pltpu.SemaphoreType.DMA((96,)),
        "local_sem": pltpu.SemaphoreType.DMA((HALVES + CHUNKS + 2,)),
        "own": panel(HALVES, PANELS),
        "tiles32": pltpu.VMEM((TILES, TILE, TILE), jnp.int32),
        "blocks": panel(TILES),
        "degs": pltpu.VMEM((TILE, TILE), F32),
        "deg_out": pltpu.VMEM((COLS, 8, TILE), F32),
        "deg_in": pltpu.VMEM((COLS - 1, 8, TILE), F32),
        "deg": pltpu.VMEM((PANELS, TILE, TILE), F32),
        "rows": pltpu.VMEM((8, TILE), jnp.int32),
        "meta": pltpu.VMEM((8, TILE), jnp.int32),
        "meta_smem": pltpu.SMEM((8, TILE), jnp.int32),
        "lists_out": pltpu.VMEM((8, TILE), jnp.int32),
        "lists_in": pltpu.VMEM((8, TILE), jnp.int32),
        "lists_smem": pltpu.SMEM((8, TILE), jnp.int32),
        "mixed": pltpu.VMEM((PANELS, TILE, 2 * TILE), F32),
        "swap_out": panel(HALVES, 8 * PANELS),
        "swap_in": panel(HALVES, 8 * PANELS),
    }
    for h in range(HALVES):
        for k in range(3):
            spec[f"fwd{h}{k}"] = panel(PANELS)
            spec[f"bwd{h}{k}"] = panel(PANELS)
        spec[f"opp{h}"] = panel(PANELS)
        spec[f"oper{h}"] = panel(ROWS * CAP)
        spec[f"pair{h}"] = panel(8 * CAP)
        spec[f"sums{h}"] = pltpu.VMEM((TILES + 1, TILE, TILE), F32)
        n = YFIRST[h]
        m = PANELS - n
        if n:
            spec[f"y1_out{h}"] = panel(3, 2 * n)
            spec[f"y1_in{h}"] = panel(3, 2 * n)
            spec[f"x2_out{h}"] = panel(n)
            spec[f"x2_in{h}"] = panel(n)
        if m:
            spec[f"x1_out{h}"] = panel(4, m)
            spec[f"x1_in{h}"] = panel(4, m)
            spec[f"y2_out{h}"] = panel(3, m)
            spec[f"y2_in{h}"] = panel(3, m)
    return spec


SCRATCH_NAMES = list(scratch_spec())


def shards(
    features, tiles, tile_rows, tile_cols, tile_count, panel_lists, self_weight, neigh_weight, bias
):
    vmem = pl.BlockSpec(memory_space=pltpu.VMEM)
    smem = pl.BlockSpec(memory_space=pltpu.SMEM)
    hbm = pl.BlockSpec(memory_space=pl.ANY)
    lists = panel_lists.reshape(1, ROWS * CAP)
    return pl.pallas_call(
        kernel,
        out_shape=jax.ShapeDtypeStruct((PANELS * TILE, 2 * TILE), BF16),
        in_specs=[hbm, hbm, vmem, smem, smem, smem, vmem, vmem, vmem, vmem],
        out_specs=vmem,
        scratch_shapes=list(scratch_spec().values()),
        compiler_params=pltpu.CompilerParams(
            collective_id=0, has_side_effects=True, vmem_limit_bytes=56 << 20
        ),
        name="sage",
    )(
        features.reshape(PANELS, TILE, 2 * TILE),
        tiles[0, 0],
        tile_rows[0],
        tile_cols[0],
        tile_count,
        lists,
        lists,
        self_weight,
        neigh_weight,
        bias.reshape(1, 2 * TILE),
    )


def solution(mesh):
    return jax.shard_map(
        shards,
        mesh=mesh,
        in_specs=(
            P(("row", "col"), None),
            P("row", "col", None, None, None),
            P("row", "col", None),
            P("row", "col", None),
            P("row", "col"),
            P("row", "col", None, None),
            P(),
            P(),
            P(),
        ),
        out_specs=P(("row", "col"), None),
        check_vma=False,
    )
```

```python
import functools

import jax
import jax.numpy as jnp
from jax import lax
from jax.experimental import pallas as pl
from jax.experimental.pallas import tpu as pltpu
from jax.sharding import PartitionSpec as P

MESH = pl.DeviceIdType.MESH
Z = 8
Y = 4
TILE = 128
HALVES = 2
PANELS = 4
TILES = 96
CAP = 2
COLS = 16
ROWS = 16
CHUNKS = 4
YFIRST = (2, 2)

F32 = jnp.float32
BF16 = jnp.bfloat16


class Sems:
    def __init__(self, send, recv):
        self.send, self.recv, self.used, self.copies = send, recv, 0, []

    def copy(self, src, dst, device):
        n = self.used
        self.used += 1
        c = pltpu.make_async_remote_copy(
            src_ref=src,
            dst_ref=dst,
            send_sem=self.send.at[n],
            recv_sem=self.recv.at[n],
            device_id=device,
            device_id_type=MESH,
        )
        self.copies.append(c)
        return c


def kernel(
    feat_ref,
    tiles_ref,
    rows_ref,
    cols_ref,
    count_ref,
    lists_ref,
    lists_vec_ref,
    ws_ref,
    wn_ref,
    bias_ref,
    out_ref,
    *scratch,
):
    s = dict(zip(SCRATCH_NAMES, scratch))
    r, c = lax.axis_index("row"), lax.axis_index("col")
    x_lo, z = r // Z, lax.rem(r, Z)
    y, x_hi, core = c // 4, lax.rem(c // 2, 2), lax.rem(c, 2)

    def z_at(d):
        return lax.rem(z + d + Z, Z)

    def at_z(d):
        return (x_lo * Z + z_at(d), c)

    def at_y(d):
        return (r, lax.rem(c + 4 * d, COLS))

    x_pair = ((1 - x_lo) * Z + z, c)
    x_far = (r, c + 2 - 4 * x_hi)
    sibling = (r, c + 1 - 2 * core)

    local = s["local_sem"]
    own_copies = []
    for h in range(HALVES):
        cp = pltpu.make_async_copy(
            feat_ref.at[:, :, pl.ds(h * TILE, TILE)], s["own"].at[h], local.at[h]
        )
        cp.start()
        own_copies.append(cp)
    per = TILES // CHUNKS
    tile_copies = []
    for k in range(CHUNKS):
        part = pl.ds(k * per, per)
        cp = pltpu.make_async_copy(
            tiles_ref.at[part], s["tiles32"].at[part], local.at[HALVES + k]
        )
        cp.start()
        tile_copies.append(cp)
    weight_copies = []
    for k, (src, dst) in enumerate(((ws_ref, s["ws"]), (wn_ref, s["wn"]))):
        cp = pltpu.make_async_copy(src, dst, local.at[HALVES + CHUNKS + 2 + k])
        cp.start()
        weight_copies.append(cp)
    s["lists_out"][...] = jnp.zeros((8, TILE), jnp.int32)
    s["lists_out"][0:CAP, 0:ROWS] = lists_vec_ref[...]

    barrier = pltpu.get_barrier_semaphore()
    peers = [at_z(1), at_z(-1), x_pair, sibling, x_far, at_y(1), at_y(2), at_y(3)]
    for peer in peers:
        pl.semaphore_signal(barrier, inc=1, device_id=peer, device_id_type=MESH)
    pl.semaphore_wait(barrier, len(peers))

    sems = Sems(s["send_sem"], s["recv_sem"])
    for cp in own_copies:
        cp.wait()

    fwd = [[s[f"fwd{h}{k}"] for k in range(3)] for h in range(HALVES)]
    bwd = [[s[f"bwd{h}{k}"] for k in range(3)] for h in range(HALVES)]
    opp = [s["opp0"], s["opp1"]]
    oper = [s["oper0"], s["oper1"]]
    ring = {}
    for h in range(HALVES):
        for k in range(4):
            for q in range(2):
                part = pl.ds(2 * q, 2)
                for way, chain in ((0, fwd[h]), (1, bwd[h])):
                    if k == 3 and q != way:
                        continue
                    src = s["own"].at[h] if k == 0 else chain[k - 1]
                    dst = chain[k] if k < 3 else opp[h]
                    ring[h, way, k, q] = sems.copy(
                        src.at[part], dst.at[part], at_z(1 - 2 * way)
                    )
    lists_copy = sems.copy(s["lists_out"], s["lists_in"], x_pair)

    lists_copy.start()

    def send(h, q):
        for way in range(2):
            ring[h, way, 0, q].start()

    send(0, 0)
    send(0, 1)
    send(1, 0)
    send(1, 1)

    pair_copies = {}

    def select(h, slot, block, dist):
        owner = x_lo * Z + z_at(dist)
        for j in range(CAP):
            mine = jnp.maximum(lists_ref[j, owner], 0)
            oper[h][owner * CAP + j] = block[mine]
        for j in range(CAP):
            theirs = jnp.maximum(s["lists_smem"][j, owner], 0)
            s[f"pair{h}"][slot * CAP + j] = block[theirs]
        cp = sems.copy(
            s[f"pair{h}"].at[pl.ds(slot * CAP, CAP)],
            oper[h].at[pl.ds(owner * CAP, CAP)],
            x_pair,
        )
        cp.start()
        pair_copies[h, slot] = cp

    live = count_ref[0, 0]
    lane = lax.broadcasted_iota(jnp.int32, (TILE, TILE), 1)
    sub = lax.broadcasted_iota(jnp.int32, (TILE, TILE), 0)
    s["rows"][...] = jnp.full((8, TILE), -1, jnp.int32)
    s["rows"][0:1, 0:TILES] = rows_ref[...]
    row_l = jnp.broadcast_to(s["rows"][0:1, :], (TILE, TILE))
    row_l = jnp.where(lane < live, row_l, -1)
    row_s = jnp.transpose(row_l.astype(F32)).astype(jnp.int32)
    prev = jnp.max(jnp.where((row_s == row_l) & (sub < lane), sub, -1), axis=0, keepdims=True)
    prev = jnp.where(prev < 0, TILES, prev)
    last = jnp.max(jnp.where(row_s == lane, sub, -1), axis=0, keepdims=True)
    last = jnp.where(last < 0, TILES, last)
    s["meta"][0:1, :] = prev
    s["meta"][1:2, :] = last
    s["meta"][2:8, :] = jnp.zeros((6, TILE), jnp.int32)
    meta_copy = pltpu.make_async_copy(s["meta"], s["meta_smem"], local.at[HALVES + CHUNKS])
    meta_copy.start()

    for h in range(HALVES):
        s[f"sums{h}"][TILES] = jnp.zeros((TILE, TILE), F32)

    ones = jnp.ones((16, TILE), BF16)

    def prepare(lo, hi):
        for k in range(CHUNKS):
            if lo <= k * per < hi:
                tile_copies[k].wait()

        def body(t, _):
            block = s["tiles32"][t].astype(F32).astype(BF16)
            s["blocks"][t] = block
            sums = lax.dot_general(
                ones, block, (((1,), (1,)), ((), ())), preferred_element_type=F32
            )
            s["degs"][pl.ds(t, 1), :] = sums[0:1, :]
            return 0

        lax.fori_loop(lo, hi, body, 0, unroll=True)

    def arrive(h, k, q):
        for way in range(2):
            if (h, way, k, q) in ring:
                ring[h, way, k, q].wait_recv()
            if (h, way, k + 1, q) in ring:
                ring[h, way, k + 1, q].start()

    def cross(h, k):
        if k < 3:
            select(h, 1 + k, fwd[h][k], -(k + 1))
            select(h, 4 + k, bwd[h][k], k + 1)
        else:
            select(h, 7, opp[h], 4)

    def base(i):
        mixed = jnp.dot(s["own"][0, i], s["ws"][0:TILE, :], preferred_element_type=F32)
        mixed += jnp.dot(s["own"][1, i], s["ws"][TILE : 2 * TILE, :], preferred_element_type=F32)
        s["mixed"][i] = mixed + bias_ref[...]

    prepare(0, 12)
    lists_copy.wait_recv()
    smem_copy = pltpu.make_async_copy(
        s["lists_in"], s["lists_smem"], local.at[HALVES + CHUNKS + 1]
    )
    smem_copy.start()
    smem_copy.wait()
    for h in range(HALVES):
        select(h, 0, s["own"].at[h], 0)

    deg = {}

    def degree0():
        q = lax.broadcasted_iota(jnp.int32, (TILE, TILE), 0)
        b = q // 8
        owner = lax.rem(b, 4) * 4 + lax.rem(b // 4, 2) * 2 + b // 8
        panel = jnp.where(lax.rem(q, 8) < PANELS, owner * PANELS + lax.rem(q, 8), -2)
        hot = (panel == row_l).astype(F32).astype(BF16)
        s["degs"][TILES:TILE, :] = jnp.zeros((TILE - TILES, TILE), F32)
        degs = jnp.dot(hot, s["degs"][...].astype(BF16), preferred_element_type=F32)
        s["deg0_out"][...] = degs.reshape(2, 2, Y, 8, TILE)
        deg[0] = sems.copy(s["deg0_out"].at[1 - core], s["deg0_in"], sibling)
        deg[0].start()

    def degree1():
        deg[0].wait_recv()
        s["deg1_out"][...] = s["deg0_out"][core] + s["deg0_in"][...]
        deg[1] = sems.copy(s["deg1_out"].at[1 - x_hi], s["deg1_in"], x_far)
        deg[1].start()

    def degree2():
        deg[1].wait_recv()
        s["deg2_out"][...] = s["deg1_out"][x_hi] + s["deg1_in"][...]
        for dy in range(1, Y):
            to = lax.rem(y + dy, Y)
            deg[2, dy] = sems.copy(s["deg2_out"].at[to], s["deg2_in"].at[dy - 1], at_y(dy))
            deg[2, dy].start()

    def degree3():
        total = s["deg2_out"][y]
        for dy in range(1, Y):
            deg[2, dy].wait_recv()
            total += s["deg2_in"][dy - 1]
        total = jnp.maximum(total, 1.0)
        wide = jnp.transpose(jnp.concatenate([total] * 16, axis=0))
        for i in range(PANELS):
            s["deg"][i] = jnp.broadcast_to(wide[:, i : i + 1], (TILE, TILE))

    def hop(h, k):
        arrive(h, k, 0)
        arrive(h, k, 1)
        cross(h, k)

    hop(0, 0)
    prepare(12, 36)
    hop(1, 0)
    prepare(36, 60)
    hop(0, 1)
    prepare(60, 84)
    hop(1, 1)
    prepare(84, 96)
    degree0()
    arrive(0, 2, 0)
    arrive(0, 2, 1)
    cross(0, 2)
    arrive(1, 2, 0)
    arrive(0, 3, 0)
    arrive(0, 3, 1)
    cross(0, 3)
    arrive(1, 2, 1)
    cross(1, 2)
    arrive(1, 3, 0)
    arrive(1, 3, 1)
    cross(1, 3)
    for cp in weight_copies:
        cp.wait()
    for i in range(PANELS):
        base(i)

    meta_copy.wait()

    def products(h, lo, hi):
        if lo == 0:
            for slot in range(8):
                pair_copies[h, slot].wait_recv()
        sums = s[f"sums{h}"]

        def body(t, _):
            value = jnp.dot(
                s["blocks"][t], oper[h][cols_ref[0, t]], preferred_element_type=F32
            )
            sums[t] = value + sums[s["meta_smem"][0, t]]
            return 0

        lax.fori_loop(lo, hi, body, 0, unroll=4)

    def owner_col(dy, dx, which):
        hi = x_hi if dx == 0 else 1 - x_hi
        return lax.rem(y + dy, Y) * 4 + hi * 2 + which

    order = [(2, 1), (2, 0), (1, 1), (1, 0), (3, 1), (3, 0), (0, 1), (0, 0)]
    swap = {}

    def partial(h, dy, dx, which, i):
        p = owner_col(dy, dx, which) * PANELS + i
        return s[f"sums{h}"][s["meta_smem"][1, p]]

    def exchange(h):
        for dy, dx in order:
            j = dy * 2 + dx

            def body(i, _):
                s["swap_out"][h, j * PANELS + i] = partial(h, dy, dx, 1 - core, i).astype(BF16)
                return 0

            lax.fori_loop(0, PANELS, body, 0, unroll=True)
            part = pl.ds(j * PANELS, PANELS)
            cp = sems.copy(s["swap_out"].at[h, part], s["swap_in"].at[h, part], sibling)
            cp.start()
            swap[h, j] = cp

    def both(h, dy, dx, i):
        j = dy * 2 + dx
        return partial(h, dy, dx, core, i) + s["swap_in"][h, j * PANELS + i].astype(F32)

    stage1, stage2 = {}, {}

    def first(h):
        n = YFIRST[h]
        m = PANELS - n
        arrived = set()

        def need(dy, dx):
            if (dy, dx) not in arrived:
                arrived.add((dy, dx))
                swap[h, dy * 2 + dx].wait_recv()

        for dy in (2, 1, 3):
            need(dy, 1)
            need(dy, 0)
            if n:
                for dx in (1, 0):
                    for i in range(n):
                        s[f"y1_out{h}"][dy - 1, dx * n + i] = both(h, dy, dx, i).astype(BF16)
                cp = sems.copy(
                    s[f"y1_out{h}"].at[dy - 1], s[f"y1_in{h}"].at[dy - 1], at_y(dy)
                )
                cp.start()
                stage1[h, dy] = cp
            if m:
                for i in range(m):
                    s[f"x1_out{h}"][dy, i] = both(h, dy, 1, n + i).astype(BF16)
                cp = sems.copy(s[f"x1_out{h}"].at[dy], s[f"x1_in{h}"].at[dy], x_far)
                cp.start()
                stage1[h, "x", dy] = cp
        need(0, 1)
        need(0, 0)
        if m:
            for i in range(m):
                s[f"x1_out{h}"][0, i] = both(h, 0, 1, n + i).astype(BF16)
            cp = sems.copy(s[f"x1_out{h}"].at[0], s[f"x1_in{h}"].at[0], x_far)
            cp.start()
            stage1[h, "x", 0] = cp

    def second(h):
        n = YFIRST[h]
        m = PANELS - n
        if m:
            for dy in (2, 1, 3):
                stage1[h, "x", dy].wait_recv()
                for i in range(m):
                    total = both(h, dy, 0, n + i) + s[f"x1_in{h}"][dy, i].astype(F32)
                    s[f"y2_out{h}"][dy - 1, i] = total.astype(BF16)
                cp = sems.copy(
                    s[f"y2_out{h}"].at[dy - 1], s[f"y2_in{h}"].at[dy - 1], at_y(dy)
                )
                cp.start()
                stage2[h, dy] = cp
        if n:
            for dy in (2, 1, 3):
                stage1[h, dy].wait_recv()
            for i in range(n):
                total = both(h, 0, 1, i)
                for dy in (2, 1, 3):
                    total += s[f"y1_in{h}"][dy - 1, n + i].astype(F32)
                s[f"x2_out{h}"][i] = total.astype(BF16)
            cp = sems.copy(s[f"x2_out{h}"], s[f"x2_in{h}"], x_far)
            cp.start()
            stage2[h, "x"] = cp

    def third(h):
        n = YFIRST[h]
        m = PANELS - n
        if m:
            stage1[h, "x", 0].wait_recv()
            for dy in (2, 1, 3):
                stage2[h, dy].wait_recv()
        if n:
            stage2[h, "x"].wait_recv()
        for i in range(PANELS):
            total = both(h, 0, 0, i)
            if i < n:
                for dy in (2, 1, 3):
                    total += s[f"y1_in{h}"][dy - 1, i].astype(F32)
                total += s[f"x2_in{h}"][i].astype(F32)
            else:
                total += s[f"x1_in{h}"][0, i - n].astype(F32)
                for dy in (2, 1, 3):
                    total += s[f"y2_in{h}"][dy - 1, i - n].astype(F32)
            mean = (total / s["deg"][i]).astype(BF16)
            s["mixed"][i] += jnp.dot(
                mean, s["wn"][h * TILE : (h + 1) * TILE, :], preferred_element_type=F32
            )

    products(0, 0, 96)
    exchange(0)
    degree1()
    first(0)
    products(1, 0, 96)
    exchange(1)
    degree2()
    first(1)
    degree3()
    second(0)
    second(1)
    third(0)
    third(1)
    for i in range(PANELS):
        out_ref[pl.ds(i * TILE, TILE), :] = jnp.maximum(s["mixed"][i], 0.0).astype(BF16)
    for cp in sems.copies:
        cp.wait_send()


def scratch_spec():
    panel = lambda *lead: pltpu.VMEM((*lead, TILE, TILE), BF16)
    spec = {
        "send_sem": pltpu.SemaphoreType.DMA((112,)),
        "recv_sem": pltpu.SemaphoreType.DMA((112,)),
        "local_sem": pltpu.SemaphoreType.DMA((HALVES + CHUNKS + 4,)),
        "own": panel(HALVES, PANELS),
        "ws": pltpu.VMEM((2 * TILE, 2 * TILE), BF16),
        "wn": pltpu.VMEM((2 * TILE, 2 * TILE), BF16),
        "tiles32": pltpu.VMEM((TILES, TILE, TILE), jnp.int32),
        "blocks": panel(TILES),
        "degs": pltpu.VMEM((TILE, TILE), F32),
        "deg0_out": pltpu.VMEM((2, 2, Y, 8, TILE), F32),
        "deg0_in": pltpu.VMEM((2, Y, 8, TILE), F32),
        "deg1_out": pltpu.VMEM((2, Y, 8, TILE), F32),
        "deg1_in": pltpu.VMEM((Y, 8, TILE), F32),
        "deg2_out": pltpu.VMEM((Y, 8, TILE), F32),
        "deg2_in": pltpu.VMEM((Y - 1, 8, TILE), F32),
        "deg": pltpu.VMEM((PANELS, TILE, TILE), F32),
        "rows": pltpu.VMEM((8, TILE), jnp.int32),
        "meta": pltpu.VMEM((8, TILE), jnp.int32),
        "meta_smem": pltpu.SMEM((8, TILE), jnp.int32),
        "lists_out": pltpu.VMEM((8, TILE), jnp.int32),
        "lists_in": pltpu.VMEM((8, TILE), jnp.int32),
        "lists_smem": pltpu.SMEM((8, TILE), jnp.int32),
        "mixed": pltpu.VMEM((PANELS, TILE, 2 * TILE), F32),
        "swap_out": panel(HALVES, 8 * PANELS),
        "swap_in": panel(HALVES, 8 * PANELS),
    }
    for h in range(HALVES):
        for k in range(3):
            spec[f"fwd{h}{k}"] = panel(PANELS)
            spec[f"bwd{h}{k}"] = panel(PANELS)
        spec[f"opp{h}"] = panel(PANELS)
        spec[f"oper{h}"] = panel(ROWS * CAP)
        spec[f"pair{h}"] = panel(8 * CAP)
        spec[f"sums{h}"] = pltpu.VMEM((TILES + 1, TILE, TILE), F32)
        n = YFIRST[h]
        m = PANELS - n
        if n:
            spec[f"y1_out{h}"] = panel(3, 2 * n)
            spec[f"y1_in{h}"] = panel(3, 2 * n)
            spec[f"x2_out{h}"] = panel(n)
            spec[f"x2_in{h}"] = panel(n)
        if m:
            spec[f"x1_out{h}"] = panel(4, m)
            spec[f"x1_in{h}"] = panel(4, m)
            spec[f"y2_out{h}"] = panel(3, m)
            spec[f"y2_in{h}"] = panel(3, m)
    return spec


SCRATCH_NAMES = list(scratch_spec())


def shards(
    features, tiles, tile_rows, tile_cols, tile_count, panel_lists, self_weight, neigh_weight, bias
):
    vmem = pl.BlockSpec(memory_space=pltpu.VMEM)
    smem = pl.BlockSpec(memory_space=pltpu.SMEM)
    hbm = pl.BlockSpec(memory_space=pl.ANY)
    lists = panel_lists[0, 0].T
    return pl.pallas_call(
        kernel,
        out_shape=jax.ShapeDtypeStruct((PANELS * TILE, 2 * TILE), BF16),
        in_specs=[hbm, hbm, vmem, smem, smem, smem, vmem, hbm, hbm, vmem],
        out_specs=vmem,
        scratch_shapes=list(scratch_spec().values()),
        compiler_params=pltpu.CompilerParams(
            collective_id=0, has_side_effects=True, vmem_limit_bytes=56 << 20
        ),
        name="sage",
    )(
        features.reshape(PANELS, TILE, 2 * TILE),
        tiles[0, 0],
        tile_rows[0],
        tile_cols[0],
        tile_count,
        lists,
        lists,
        self_weight,
        neigh_weight,
        bias.reshape(1, 2 * TILE),
    )


def solution(mesh):
    return jax.shard_map(
        shards,
        mesh=mesh,
        in_specs=(
            P(("row", "col"), None),
            P("row", "col", None, None, None),
            P("row", "col", None),
            P("row", "col", None),
            P("row", "col"),
            P("row", "col", None, None),
            P(),
            P(),
            P(),
        ),
        out_specs=P(("row", "col"), None),
        check_vma=False,
    )
```

```python
import functools

import jax
import jax.numpy as jnp
from jax import lax
from jax.experimental import pallas as pl
from jax.experimental.pallas import tpu as pltpu
from jax.sharding import PartitionSpec as P

MESH = pl.DeviceIdType.MESH
Z = 8
Y = 4
TILE = 128
HALVES = 2
PANELS = 4
TILES = 96
CAP = 2
COLS = 16
ROWS = 16
CHUNKS = 4
YFIRST = (2, 2)

F32 = jnp.float32
BF16 = jnp.bfloat16


class Sems:
    def __init__(self, send, recv):
        self.send, self.recv, self.used, self.copies = send, recv, 0, []

    def copy(self, src, dst, device):
        n = self.used
        self.used += 1
        c = pltpu.make_async_remote_copy(
            src_ref=src,
            dst_ref=dst,
            send_sem=self.send.at[n],
            recv_sem=self.recv.at[n],
            device_id=device,
            device_id_type=MESH,
        )
        self.copies.append(c)
        return c


def kernel(
    feat_ref,
    tiles_ref,
    rows_hbm,
    cols_hbm,
    count_hbm,
    lists_hbm,
    ws_hbm,
    wn_hbm,
    bias_hbm,
    out_ref,
    *scratch,
):
    s = dict(zip(SCRATCH_NAMES, scratch))
    r, c = lax.axis_index("row"), lax.axis_index("col")
    x_lo, z = r // Z, lax.rem(r, Z)
    y, x_hi, core = c // 4, lax.rem(c // 2, 2), lax.rem(c, 2)

    def z_at(d):
        return lax.rem(z + d + Z, Z)

    def at_z(d):
        return (x_lo * Z + z_at(d), c)

    def at_y(d):
        return (r, lax.rem(c + 4 * d + COLS, COLS))

    x_pair = ((1 - x_lo) * Z + z, c)
    x_far = (r, c + 2 - 4 * x_hi)
    sibling = (r, c + 1 - 2 * core)

    local = s["local_sem"]
    own_copies = []
    for h in range(HALVES):
        cp = pltpu.make_async_copy(
            feat_ref.at[:, :, pl.ds(h * TILE, TILE)], s["own"].at[h], local.at[h]
        )
        cp.start()
        own_copies.append(cp)
    small_copies, weight_copies = [], []
    for k, (src, dst) in enumerate(
        (
            (lists_hbm, s["lists_vec"]),
            (lists_hbm, s["lists"]),
            (rows_hbm, s["rows_vec"]),
            (count_hbm, s["count"]),
            (cols_hbm, s["cols"]),
            (bias_hbm, s["bias"]),
            (ws_hbm, s["ws"]),
            (wn_hbm, s["wn"]),
        )
    ):
        cp = pltpu.make_async_copy(src, dst, local.at[HALVES + CHUNKS + 2 + k])
        cp.start()
        (small_copies if k < 5 else weight_copies).append(cp)
    per = TILES // CHUNKS
    tile_copies = []
    for k in range(CHUNKS):
        part = pl.ds(k * per, per)
        cp = pltpu.make_async_copy(
            tiles_ref.at[part], s["tiles32"].at[part], local.at[HALVES + k]
        )
        cp.start()
        tile_copies.append(cp)

    barrier = pltpu.get_barrier_semaphore()
    peers = [at_z(1), at_z(-1), x_pair, sibling, x_far, at_y(1), at_y(2), at_y(3)]
    for peer in peers:
        pl.semaphore_signal(barrier, inc=1, device_id=peer, device_id_type=MESH)
    pl.semaphore_wait(barrier, len(peers))

    sems = Sems(s["send_sem"], s["recv_sem"])
    for cp in own_copies:
        cp.wait()

    fwd = [[s[f"fwd{h}{k}"] for k in range(3)] for h in range(HALVES)]
    bwd = [[s[f"bwd{h}{k}"] for k in range(3)] for h in range(HALVES)]
    opp = [s["opp0"], s["opp1"]]
    oper = [s["oper0"], s["oper1"]]
    ring = {}
    for h in range(HALVES):
        for k in range(4):
            for q in range(2):
                part = pl.ds(2 * q, 2)
                for way, chain in ((0, fwd[h]), (1, bwd[h])):
                    if k == 3 and q != way:
                        continue
                    src = s["own"].at[h] if k == 0 else chain[k - 1]
                    dst = chain[k] if k < 3 else opp[h]
                    ring[h, way, k, q] = sems.copy(
                        src.at[part], dst.at[part], at_z(1 - 2 * way)
                    )
    lists_copy = sems.copy(s["lists_out"], s["lists_in"], x_pair)

    for cp in small_copies:
        cp.wait()
    lists_ref, cols_ref = s["lists"], s["cols"]

    def send(h, q):
        for way in range(2):
            ring[h, way, 0, q].start()

    send(0, 0)
    send(0, 1)
    s["lists_out"][...] = jnp.zeros((8, TILE), jnp.int32)
    s["lists_out"][0:CAP, 0:ROWS] = s["lists_vec"][...]
    lists_copy.start()
    send(1, 0)
    send(1, 1)

    pair_copies = {}

    def select(h, slot, block, dist):
        owner = x_lo * Z + z_at(dist)
        for j in range(CAP):
            mine = jnp.maximum(lists_ref[j, owner], 0)
            oper[h][owner * CAP + j] = block[mine]
        for j in range(CAP):
            theirs = jnp.maximum(s["lists_smem"][j, owner], 0)
            s[f"pair{h}"][slot * CAP + j] = block[theirs]
        cp = sems.copy(
            s[f"pair{h}"].at[pl.ds(slot * CAP, CAP)],
            oper[h].at[pl.ds(owner * CAP, CAP)],
            x_pair,
        )
        cp.start()
        pair_copies[h, slot] = cp

    live = s["count"][0, 0]
    lane = lax.broadcasted_iota(jnp.int32, (TILE, TILE), 1)
    sub = lax.broadcasted_iota(jnp.int32, (TILE, TILE), 0)
    s["rows"][...] = jnp.full((8, TILE), -1, jnp.int32)
    s["rows"][0:1, 0:TILES] = s["rows_vec"][...]
    row_l = jnp.broadcast_to(s["rows"][0:1, :], (TILE, TILE))
    row_l = jnp.where(lane < live, row_l, -1)
    row_s = jnp.transpose(row_l.astype(F32)).astype(jnp.int32)
    prev = jnp.max(jnp.where((row_s == row_l) & (sub < lane), sub, -1), axis=0, keepdims=True)
    prev = jnp.where(prev < 0, TILES, prev)
    last = jnp.max(jnp.where(row_s == lane, sub, -1), axis=0, keepdims=True)
    last = jnp.where(last < 0, TILES, last)
    s["meta"][0:1, :] = prev
    s["meta"][1:2, :] = last
    s["meta"][2:8, :] = jnp.zeros((6, TILE), jnp.int32)
    meta_copy = pltpu.make_async_copy(s["meta"], s["meta_smem"], local.at[HALVES + CHUNKS])
    meta_copy.start()

    for h in range(HALVES):
        s[f"sums{h}"][TILES] = jnp.zeros((TILE, TILE), F32)

    ones = jnp.ones((16, TILE), BF16)

    def prepare(lo, hi):
        for k in range(CHUNKS):
            if lo <= k * per < hi:
                tile_copies[k].wait()

        def body(t, _):
            block = s["tiles32"][t].astype(F32).astype(BF16)
            s["blocks"][t] = block
            sums = lax.dot_general(
                ones, block, (((1,), (1,)), ((), ())), preferred_element_type=F32
            )
            s["degs"][pl.ds(t, 1), :] = sums[0:1, :]
            return 0

        lax.fori_loop(lo, hi, body, 0, unroll=True)

    def arrive(h, k, q):
        for way in range(2):
            if (h, way, k, q) in ring:
                ring[h, way, k, q].wait_recv()
            if (h, way, k + 1, q) in ring:
                ring[h, way, k + 1, q].start()

    def cross(h, k):
        if k < 3:
            select(h, 1 + k, fwd[h][k], -(k + 1))
            select(h, 4 + k, bwd[h][k], k + 1)
        else:
            select(h, 7, opp[h], 4)

    def base(i):
        mixed = jnp.dot(s["own"][0, i], s["ws"][0:TILE, :], preferred_element_type=F32)
        mixed += jnp.dot(s["own"][1, i], s["ws"][TILE : 2 * TILE, :], preferred_element_type=F32)
        s["mixed"][i] = mixed + s["bias"][...]

    prepare(0, 12)
    lists_copy.wait_recv()
    smem_copy = pltpu.make_async_copy(
        s["lists_in"], s["lists_smem"], local.at[HALVES + CHUNKS + 1]
    )
    smem_copy.start()
    smem_copy.wait()
    for h in range(HALVES):
        select(h, 0, s["own"].at[h], 0)

    deg = {}

    def degree0():
        q = lax.broadcasted_iota(jnp.int32, (TILE, TILE), 0)
        b = q // 8
        owner = lax.rem(b, 4) * 4 + lax.rem(b // 4, 2) * 2 + b // 8
        panel = jnp.where(lax.rem(q, 8) < PANELS, owner * PANELS + lax.rem(q, 8), -2)
        hot = (panel == row_l).astype(F32).astype(BF16)
        s["degs"][TILES:TILE, :] = jnp.zeros((TILE - TILES, TILE), F32)
        degs = jnp.dot(hot, s["degs"][...].astype(BF16), preferred_element_type=F32)
        s["deg0_out"][...] = degs.reshape(2, 2, Y, 8, TILE)
        deg[0] = sems.copy(s["deg0_out"].at[1 - core], s["deg0_in"], sibling)
        deg[0].start()

    def degree1():
        deg[0].wait_recv()
        s["deg1_out"][...] = s["deg0_out"][core] + s["deg0_in"][...]
        deg[1] = sems.copy(s["deg1_out"].at[1 - x_hi], s["deg1_in"], x_far)
        deg[1].start()

    def degree2():
        deg[1].wait_recv()
        s["deg2_out"][...] = s["deg1_out"][x_hi] + s["deg1_in"][...]
        for dy in range(1, Y):
            to = lax.rem(y + dy, Y)
            deg[2, dy] = sems.copy(s["deg2_out"].at[to], s["deg2_in"].at[dy - 1], at_y(dy))
            deg[2, dy].start()

    def degree3():
        total = s["deg2_out"][y]
        for dy in range(1, Y):
            deg[2, dy].wait_recv()
            total += s["deg2_in"][dy - 1]
        total = jnp.maximum(total, 1.0)
        wide = jnp.transpose(jnp.concatenate([total] * 16, axis=0))
        for i in range(PANELS):
            s["deg"][i] = jnp.broadcast_to(wide[:, i : i + 1], (TILE, TILE))

    arrive(0, 0, 0)
    arrive(0, 0, 1)
    cross(0, 0)
    prepare(12, 36)
    arrive(1, 0, 0)
    arrive(1, 0, 1)
    cross(1, 0)
    prepare(36, 60)
    arrive(0, 1, 0)
    arrive(0, 1, 1)
    cross(0, 1)
    prepare(60, 84)
    arrive(1, 1, 0)
    arrive(1, 1, 1)
    cross(1, 1)
    prepare(84, 96)
    degree0()
    arrive(0, 2, 0)
    arrive(0, 2, 1)
    cross(0, 2)
    arrive(0, 3, 0)
    arrive(0, 3, 1)
    cross(0, 3)
    arrive(1, 2, 0)
    arrive(1, 2, 1)
    cross(1, 2)
    for cp in weight_copies:
        cp.wait()
    for i in range(PANELS):
        base(i)
    meta_copy.wait()

    def products(h, lo, hi):
        if lo == 0:
            for slot in range(8):
                pair_copies[h, slot].wait_recv()
        sums = s[f"sums{h}"]

        def body(t, _):
            value = jnp.dot(
                s["blocks"][t], oper[h][cols_ref[0, t]], preferred_element_type=F32
            )
            sums[t] = value + sums[s["meta_smem"][0, t]]
            return 0

        lax.fori_loop(lo, hi, body, 0, unroll=24)

    def owner_col(dy, dx, which):
        hi = x_hi if dx == 0 else 1 - x_hi
        return lax.rem(y + dy, Y) * 4 + hi * 2 + which

    order = [(2, 1), (2, 0), (1, 1), (1, 0), (3, 1), (3, 0), (0, 1), (0, 0)]
    swap = {}

    def partial(h, dy, dx, which, i):
        p = owner_col(dy, dx, which) * PANELS + i
        return s[f"sums{h}"][s["meta_smem"][1, p]]

    def exchange(h):
        for dy, dx in order:
            j = dy * 2 + dx

            def body(i, _):
                s["swap_out"][h, j * PANELS + i] = partial(h, dy, dx, 1 - core, i).astype(BF16)
                return 0

            lax.fori_loop(0, PANELS, body, 0, unroll=True)
            part = pl.ds(j * PANELS, PANELS)
            cp = sems.copy(s["swap_out"].at[h, part], s["swap_in"].at[h, part], sibling)
            cp.start()
            swap[h, j] = cp

    def both(h, dy, dx, i):
        j = dy * 2 + dx
        return partial(h, dy, dx, core, i) + s["swap_in"][h, j * PANELS + i].astype(F32)

    stage1, stage2, arrived = {}, {}, set()

    def need(h, dy):
        for dx in (1, 0):
            if (h, dy, dx) not in arrived:
                arrived.add((h, dy, dx))
                swap[h, dy * 2 + dx].wait_recv()

    def post(stage, key, out, into, device):
        cp = sems.copy(out, into, device)
        cp.start()
        stage[key] = cp

    def first(h):
        n = YFIRST[h]
        m = PANELS - n
        far_out, far_in = s[f"far_out{h}"], s[f"far_in{h}"]
        y1_out, y1_in = s[f"y1_out{h}"], s[f"y1_in{h}"]
        for dy in (2, 1, 3, 0):
            need(h, dy)
            if dy == 2:
                for side in range(2):
                    for i in range(n):
                        far_out[side, i] = both(h, 2, side, i).astype(BF16)
                    post(stage1, (h, "far", side), far_out.at[side], far_in.at[side], at_y(1 - 2 * side))
            elif dy:
                side = dy // 2
                dx = 1 - side
                for i in range(n):
                    y1_out[side, dx, i] = both(h, dy, dx, i).astype(BF16)
                post(stage1, (h, "y", side, dx), y1_out.at[side, dx], y1_in.at[side, dx], at_y(1 - 2 * side))
            for i in range(m):
                s[f"x1_out{h}"][dy, i] = both(h, dy, 1, n + i).astype(BF16)
            if m:
                post(stage1, (h, "x", dy), s[f"x1_out{h}"].at[dy], s[f"x1_in{h}"].at[dy], x_far)

    def middle(h):
        n = YFIRST[h]
        y1_out, y1_in = s[f"y1_out{h}"], s[f"y1_in{h}"]
        for side in range(2):
            stage1[h, "far", side].wait_recv()
            dy, dx = 1 + 2 * side, side
            for i in range(n):
                total = both(h, dy, dx, i) + s[f"far_in{h}"][side, i].astype(F32)
                y1_out[side, dx, i] = total.astype(BF16)
            post(stage1, (h, "y", side, dx), y1_out.at[side, dx], y1_in.at[side, dx], at_y(1 - 2 * side))

    def second(h):
        n = YFIRST[h]
        m = PANELS - n
        if m:
            for dy in (2, 1, 3):
                stage1[h, "x", dy].wait_recv()
                for i in range(m):
                    total = both(h, dy, 0, n + i) + s[f"x1_in{h}"][dy, i].astype(F32)
                    s[f"y2_out{h}"][dy - 1, i] = total.astype(BF16)
                post(stage2, (h, dy), s[f"y2_out{h}"].at[dy - 1], s[f"y2_in{h}"].at[dy - 1], at_y(dy))
        for side in range(2):
            stage1[h, "y", side, 1].wait_recv()
        for i in range(n):
            total = both(h, 0, 1, i)
            for side in range(2):
                total += s[f"y1_in{h}"][side, 1, i].astype(F32)
            s[f"x2_out{h}"][i] = total.astype(BF16)
        post(stage2, (h, "x"), s[f"x2_out{h}"], s[f"x2_in{h}"], x_far)

    def third(h):
        n = YFIRST[h]
        m = PANELS - n
        if m:
            stage1[h, "x", 0].wait_recv()
            for dy in (2, 1, 3):
                stage2[h, dy].wait_recv()
        for side in range(2):
            stage1[h, "y", side, 0].wait_recv()
        stage2[h, "x"].wait_recv()
        for i in range(PANELS):
            total = both(h, 0, 0, i)
            if i < n:
                for side in range(2):
                    total += s[f"y1_in{h}"][side, 0, i].astype(F32)
                total += s[f"x2_in{h}"][i].astype(F32)
            else:
                total += s[f"x1_in{h}"][0, i - n].astype(F32)
                for dy in (2, 1, 3):
                    total += s[f"y2_in{h}"][dy - 1, i - n].astype(F32)
            mean = (total / s["deg"][i]).astype(BF16)
            s["mixed"][i] += jnp.dot(
                mean, s["wn"][h * TILE : (h + 1) * TILE, :], preferred_element_type=F32
            )

    products(0, 0, 48)
    arrive(1, 3, 0)
    arrive(1, 3, 1)
    cross(1, 3)
    products(0, 48, 96)
    exchange(0)
    degree1()
    first(0)
    products(1, 0, 48)
    middle(0)
    products(1, 48, 96)
    exchange(1)
    degree2()
    first(1)
    degree3()
    middle(1)
    second(0)
    second(1)
    third(0)
    third(1)
    for i in range(PANELS):
        out_ref[pl.ds(i * TILE, TILE), :] = jnp.maximum(s["mixed"][i], 0.0).astype(BF16)
    for cp in sems.copies:
        cp.wait_send()


def scratch_spec():
    panel = lambda *lead: pltpu.VMEM((*lead, TILE, TILE), BF16)
    spec = {
        "send_sem": pltpu.SemaphoreType.DMA((112,)),
        "recv_sem": pltpu.SemaphoreType.DMA((112,)),
        "local_sem": pltpu.SemaphoreType.DMA((HALVES + CHUNKS + 10,)),
        "own": panel(HALVES, PANELS),
        "lists_vec": pltpu.VMEM((CAP, ROWS), jnp.int32),
        "lists": pltpu.SMEM((CAP, ROWS), jnp.int32),
        "rows_vec": pltpu.VMEM((1, TILES), jnp.int32),
        "count": pltpu.SMEM((1, 1), jnp.int32),
        "cols": pltpu.SMEM((1, TILES), jnp.int32),
        "bias": pltpu.VMEM((1, 2 * TILE), F32),
        "ws": pltpu.VMEM((2 * TILE, 2 * TILE), BF16),
        "wn": pltpu.VMEM((2 * TILE, 2 * TILE), BF16),
        "tiles32": pltpu.VMEM((TILES, TILE, TILE), jnp.int32),
        "blocks": panel(TILES),
        "degs": pltpu.VMEM((TILE, TILE), F32),
        "deg0_out": pltpu.VMEM((2, 2, Y, 8, TILE), F32),
        "deg0_in": pltpu.VMEM((2, Y, 8, TILE), F32),
        "deg1_out": pltpu.VMEM((2, Y, 8, TILE), F32),
        "deg1_in": pltpu.VMEM((Y, 8, TILE), F32),
        "deg2_out": pltpu.VMEM((Y, 8, TILE), F32),
        "deg2_in": pltpu.VMEM((Y - 1, 8, TILE), F32),
        "deg": pltpu.VMEM((PANELS, TILE, TILE), F32),
        "rows": pltpu.VMEM((8, TILE), jnp.int32),
        "meta": pltpu.VMEM((8, TILE), jnp.int32),
        "meta_smem": pltpu.SMEM((8, TILE), jnp.int32),
        "lists_out": pltpu.VMEM((8, TILE), jnp.int32),
        "lists_in": pltpu.VMEM((8, TILE), jnp.int32),
        "lists_smem": pltpu.SMEM((8, TILE), jnp.int32),
        "mixed": pltpu.VMEM((PANELS, TILE, 2 * TILE), F32),
        "swap_out": panel(HALVES, 8 * PANELS),
        "swap_in": panel(HALVES, 8 * PANELS),
    }
    for h in range(HALVES):
        for k in range(3):
            spec[f"fwd{h}{k}"] = panel(PANELS)
            spec[f"bwd{h}{k}"] = panel(PANELS)
        spec[f"opp{h}"] = panel(PANELS)
        spec[f"oper{h}"] = panel(ROWS * CAP)
        spec[f"pair{h}"] = panel(8 * CAP)
        spec[f"sums{h}"] = pltpu.VMEM((TILES + 1, TILE, TILE), F32)
        n = YFIRST[h]
        m = PANELS - n
        for end in ("out", "in"):
            spec[f"far_{end}{h}"] = panel(2, n)
            spec[f"y1_{end}{h}"] = panel(2, 2, n)
            spec[f"x2_{end}{h}"] = panel(n)
        if m:
            spec[f"x1_out{h}"] = panel(4, m)
            spec[f"x1_in{h}"] = panel(4, m)
            spec[f"y2_out{h}"] = panel(3, m)
            spec[f"y2_in{h}"] = panel(3, m)
    return spec


SCRATCH_NAMES = list(scratch_spec())


def shards(
    features, tiles, tile_rows, tile_cols, tile_count, panel_lists, self_weight, neigh_weight, bias
):
    vmem = pl.BlockSpec(memory_space=pltpu.VMEM)
    hbm = pl.BlockSpec(memory_space=pltpu.HBM)
    lists = panel_lists[0, 0].T
    return pl.pallas_call(
        kernel,
        out_shape=jax.ShapeDtypeStruct((PANELS * TILE, 2 * TILE), BF16),
        in_specs=[hbm] * 9,
        out_specs=vmem,
        scratch_shapes=list(scratch_spec().values()),
        compiler_params=pltpu.CompilerParams(
            collective_id=0, has_side_effects=True, vmem_limit_bytes=56 << 20
        ),
        name="sage",
    )(
        features.reshape(PANELS, TILE, 2 * TILE),
        tiles[0, 0],
        tile_rows[0],
        tile_cols[0],
        tile_count,
        lists,
        self_weight,
        neigh_weight,
        bias.reshape(1, 2 * TILE),
    )


def solution(mesh):
    return jax.shard_map(
        shards,
        mesh=mesh,
        in_specs=(
            P(("row", "col"), None),
            P("row", "col", None, None, None),
            P("row", "col", None),
            P("row", "col", None),
            P("row", "col"),
            P("row", "col", None, None),
            P(),
            P(),
            P(),
        ),
        out_specs=P(("row", "col"), None),
        check_vma=False,
    )
```

```python
import functools

import jax
import jax.numpy as jnp
from jax import lax
from jax.experimental import pallas as pl
from jax.experimental.pallas import tpu as pltpu
from jax.sharding import PartitionSpec as P

MESH = pl.DeviceIdType.MESH
Z = 8
Y = 4
TILE = 128
HALVES = 2
PANELS = 4
TILES = 96
CAP = 2
COLS = 16
ROWS = 16
CHUNKS = 4
YFIRST = (2, 2)

F32 = jnp.float32
BF16 = jnp.bfloat16


class Sems:
    def __init__(self, send, recv):
        self.send, self.recv, self.used, self.copies = send, recv, 0, []

    def copy(self, src, dst, device):
        n = self.used
        self.used += 1
        c = pltpu.make_async_remote_copy(
            src_ref=src,
            dst_ref=dst,
            send_sem=self.send.at[n],
            recv_sem=self.recv.at[n],
            device_id=device,
            device_id_type=MESH,
        )
        self.copies.append(c)
        return c

    def sent(self):
        for c in self.copies:
            c.wait_send()
        self.copies = []


def kernel(
    feat_ref,
    tiles_ref,
    rows_hbm,
    cols_hbm,
    count_hbm,
    lists_hbm,
    ws_hbm,
    wn_hbm,
    bias_hbm,
    out_ref,
    *scratch,
):
    s = dict(zip(SCRATCH_NAMES, scratch))
    r, c = lax.axis_index("row"), lax.axis_index("col")
    x_lo, z = r // Z, lax.rem(r, Z)
    y, x_hi, core = c // 4, lax.rem(c // 2, 2), lax.rem(c, 2)

    def z_at(d):
        return lax.rem(z + d + Z, Z)

    def at_z(d):
        return (x_lo * Z + z_at(d), c)

    def at_y(d):
        return (r, lax.rem(c + 4 * d + COLS, COLS))

    x_pair = ((1 - x_lo) * Z + z, c)
    x_far = (r, c + 2 - 4 * x_hi)
    sibling = (r, c + 1 - 2 * core)

    barrier = pltpu.get_barrier_semaphore()
    peers = [at_z(1), at_z(-1), x_pair, sibling, x_far, at_y(1), at_y(2), at_y(3)]
    for peer in peers:
        pl.semaphore_signal(barrier, inc=1, device_id=peer, device_id_type=MESH)

    local = s["local_sem"]
    own_copies = []
    for h in range(HALVES):
        cp = pltpu.make_async_copy(
            feat_ref.at[:, :, pl.ds(h * TILE, TILE)], s["own"].at[h], local.at[h]
        )
        cp.start()
        own_copies.append(cp)
    small_copies, weight_copies = [], []
    for k, (src, dst) in enumerate(
        (
            (lists_hbm, s["lists_vec"]),
            (lists_hbm, s["lists"]),
            (rows_hbm, s["rows_vec"]),
            (count_hbm, s["count"]),
            (cols_hbm, s["cols"]),
            (bias_hbm, s["bias"]),
            (ws_hbm, s["ws"]),
            (wn_hbm, s["wn"]),
        )
    ):
        cp = pltpu.make_async_copy(src, dst, local.at[HALVES + CHUNKS + 2 + k])
        cp.start()
        (small_copies if k < 5 else weight_copies).append(cp)
    per = TILES // CHUNKS

    pl.semaphore_wait(barrier, len(peers))

    sems = Sems(s["send_sem"], s["recv_sem"])
    for cp in own_copies:
        cp.wait()

    fwd = [[s[f"fwd{h}{k}"] for k in range(3)] for h in range(HALVES)]
    bwd = [[s[f"bwd{h}{k}"] for k in range(3)] for h in range(HALVES)]
    opp = [s["opp0"], s["opp1"]]
    oper = [s["oper0"], s["oper1"]]
    ring = {}
    for h in range(HALVES):
        for k in range(4):
            for q in range(2):
                part = pl.ds(2 * q, 2)
                for way, chain in ((0, fwd[h]), (1, bwd[h])):
                    if k == 3 and q != way:
                        continue
                    src = s["own"].at[h] if k == 0 else chain[k - 1]
                    dst = chain[k] if k < 3 else opp[h]
                    ring[h, way, k, q] = sems.copy(
                        src.at[part], dst.at[part], at_z(1 - 2 * way)
                    )
    lists_copy = sems.copy(s["lists_out"], s["lists_in"], x_pair)

    for cp in small_copies:
        cp.wait()
    lists_ref, cols_ref = s["lists"], s["cols"]

    def send(h, q):
        for way in range(2):
            ring[h, way, 0, q].start()

    send(0, 0)
    send(0, 1)
    s["lists_out"][...] = jnp.zeros((8, TILE), jnp.int32)
    s["lists_out"][0:CAP, 0:ROWS] = s["lists_vec"][...]
    lists_copy.start()
    send(1, 0)
    send(1, 1)
    tile_copies = []
    for k in range(CHUNKS):
        part = pl.ds(k * per, per)
        cp = pltpu.make_async_copy(
            tiles_ref.at[part], s["tiles32"].at[part], local.at[HALVES + k]
        )
        cp.start()
        tile_copies.append(cp)

    pair_copies = {}

    def select(h, slot, block, dist):
        owner = x_lo * Z + z_at(dist)
        for j in range(CAP):
            mine = jnp.maximum(lists_ref[j, owner], 0)
            oper[h][owner * CAP + j] = block[mine]
        for j in range(CAP):
            theirs = jnp.maximum(s["lists_smem"][j, owner], 0)
            s[f"pair{h}"][slot * CAP + j] = block[theirs]
        cp = sems.copy(
            s[f"pair{h}"].at[pl.ds(slot * CAP, CAP)],
            oper[h].at[pl.ds(owner * CAP, CAP)],
            x_pair,
        )
        cp.start()
        pair_copies[h, slot] = cp

    live = s["count"][0, 0]
    lane = lax.broadcasted_iota(jnp.int32, (TILE, TILE), 1)
    sub = lax.broadcasted_iota(jnp.int32, (TILE, TILE), 0)
    s["rows"][...] = jnp.full((8, TILE), -1, jnp.int32)
    s["rows"][0:1, 0:TILES] = s["rows_vec"][...]
    row_l = jnp.broadcast_to(s["rows"][0:1, :], (TILE, TILE))
    row_l = jnp.where(lane < live, row_l, -1)
    row_s = jnp.transpose(row_l.astype(F32)).astype(jnp.int32)
    prev = jnp.max(jnp.where((row_s == row_l) & (sub < lane), sub, -1), axis=0, keepdims=True)
    prev = jnp.where(prev < 0, TILES, prev)
    last = jnp.max(jnp.where(row_s == lane, sub, -1), axis=0, keepdims=True)
    last = jnp.where(last < 0, TILES, last)
    s["meta"][0:1, :] = prev
    s["meta"][1:2, :] = last
    s["meta"][2:8, :] = jnp.zeros((6, TILE), jnp.int32)
    meta_copy = pltpu.make_async_copy(s["meta"], s["meta_smem"], local.at[HALVES + CHUNKS])
    meta_copy.start()

    for h in range(HALVES):
        s[f"sums{h}"][TILES] = jnp.zeros((TILE, TILE), F32)

    ones = jnp.ones((16, TILE), BF16)

    def prepare(lo, hi):
        for k in range(CHUNKS):
            if lo <= k * per < hi:
                tile_copies[k].wait()

        def body(t, _):
            block = s["tiles32"][t].astype(F32).astype(BF16)
            s["blocks"][t] = block
            sums = lax.dot_general(
                ones, block, (((1,), (1,)), ((), ())), preferred_element_type=F32
            )
            s["degs"][pl.ds(t, 1), :] = sums[0:1, :]
            return 0

        lax.fori_loop(lo, hi, body, 0, unroll=True)

    def arrive(h, k, q):
        for way in range(2):
            if (h, way, k, q) in ring:
                ring[h, way, k, q].wait_recv()
            if (h, way, k + 1, q) in ring:
                ring[h, way, k + 1, q].start()

    def cross(h, k):
        if k < 3:
            select(h, 1 + k, fwd[h][k], -(k + 1))
            select(h, 4 + k, bwd[h][k], k + 1)
        else:
            select(h, 7, opp[h], 4)

    def base(i):
        mixed = jnp.dot(s["own"][0, i], s["ws"][0:TILE, :], preferred_element_type=F32)
        mixed += jnp.dot(s["own"][1, i], s["ws"][TILE : 2 * TILE, :], preferred_element_type=F32)
        s["mixed"][i] = mixed + s["bias"][...]

    prepare(0, 12)
    lists_copy.wait_recv()
    smem_copy = pltpu.make_async_copy(
        s["lists_in"], s["lists_smem"], local.at[HALVES + CHUNKS + 1]
    )
    smem_copy.start()
    smem_copy.wait()
    for h in range(HALVES):
        select(h, 0, s["own"].at[h], 0)

    deg = {}

    def degree0():
        q = lax.broadcasted_iota(jnp.int32, (TILE, TILE), 0)
        b = q // 8
        owner = lax.rem(b, 4) * 4 + lax.rem(b // 4, 2) * 2 + b // 8
        panel = jnp.where(lax.rem(q, 8) < PANELS, owner * PANELS + lax.rem(q, 8), -2)
        hot = (panel == row_l).astype(F32).astype(BF16)
        s["degs"][TILES:TILE, :] = jnp.zeros((TILE - TILES, TILE), F32)
        degs = jnp.dot(hot, s["degs"][...].astype(BF16), preferred_element_type=F32)
        s["deg0_out"][...] = degs.reshape(2, 2, Y, 8, TILE)
        deg[0] = sems.copy(s["deg0_out"].at[1 - core], s["deg0_in"], sibling)
        deg[0].start()

    def degree1():
        deg[0].wait_recv()
        s["deg1_out"][...] = s["deg0_out"][core] + s["deg0_in"][...]
        deg[1] = sems.copy(s["deg1_out"].at[1 - x_hi], s["deg1_in"], x_far)
        deg[1].start()

    def degree2():
        deg[1].wait_recv()
        s["deg2_out"][...] = s["deg1_out"][x_hi] + s["deg1_in"][...]
        for dy in range(1, Y):
            to = lax.rem(y + dy, Y)
            deg[2, dy] = sems.copy(s["deg2_out"].at[to], s["deg2_in"].at[dy - 1], at_y(dy))
            deg[2, dy].start()

    def degree3():
        total = s["deg2_out"][y]
        for dy in range(1, Y):
            deg[2, dy].wait_recv()
            total += s["deg2_in"][dy - 1]
        total = jnp.maximum(total, 1.0)
        wide = jnp.transpose(jnp.concatenate([total] * 16, axis=0))
        for i in range(PANELS):
            s["deg"][i] = jnp.broadcast_to(wide[:, i : i + 1], (TILE, TILE))

    arrive(0, 0, 0)
    arrive(0, 0, 1)
    cross(0, 0)
    prepare(12, 36)
    arrive(1, 0, 0)
    arrive(1, 0, 1)
    cross(1, 0)
    prepare(36, 60)
    arrive(0, 1, 0)
    arrive(0, 1, 1)
    cross(0, 1)
    prepare(60, 84)
    arrive(1, 1, 0)
    arrive(1, 1, 1)
    cross(1, 1)
    prepare(84, 96)
    degree0()
    arrive(0, 2, 0)
    arrive(0, 2, 1)
    cross(0, 2)
    arrive(0, 3, 0)
    arrive(0, 3, 1)
    cross(0, 3)
    arrive(1, 2, 0)
    arrive(1, 2, 1)
    cross(1, 2)
    for cp in weight_copies:
        cp.wait()
    for i in range(PANELS):
        base(i)
    meta_copy.wait()

    def products(h, lo, hi):
        if lo == 0:
            for slot in range(8):
                pair_copies[h, slot].wait_recv()
        sums = s[f"sums{h}"]

        def body(t, _):
            value = jnp.dot(
                s["blocks"][t], oper[h][cols_ref[0, t]], preferred_element_type=F32
            )
            sums[t] = value + sums[s["meta_smem"][0, t]]
            return 0

        lax.fori_loop(lo, hi, body, 0, unroll=24)

    def owner_col(dy, dx, which):
        hi = x_hi if dx == 0 else 1 - x_hi
        return lax.rem(y + dy, Y) * 4 + hi * 2 + which

    order = [(2, 1), (2, 0), (1, 1), (1, 0), (3, 1), (3, 0), (0, 1), (0, 0)]
    swap = {}

    def partial(h, dy, dx, which, i):
        p = owner_col(dy, dx, which) * PANELS + i
        return s[f"sums{h}"][s["meta_smem"][1, p]]

    def exchange(h):
        for dy, dx in order:
            j = dy * 2 + dx

            def body(i, _):
                s["swap_out"][h, j * PANELS + i] = partial(h, dy, dx, 1 - core, i).astype(BF16)
                return 0

            lax.fori_loop(0, PANELS, body, 0, unroll=True)
            part = pl.ds(j * PANELS, PANELS)
            cp = sems.copy(s["swap_out"].at[h, part], s["swap_in"].at[h, part], sibling)
            cp.start()
            swap[h, j] = cp

    def both(h, dy, dx, i):
        j = dy * 2 + dx
        return partial(h, dy, dx, core, i) + s["swap_in"][h, j * PANELS + i].astype(F32)

    stage1, stage2, arrived, hidden_copies = {}, {}, set(), []

    def need(h, dy):
        for dx in (1, 0):
            if (h, dy, dx) not in arrived:
                arrived.add((h, dy, dx))
                swap[h, dy * 2 + dx].wait_recv()

    def post(stage, key, out, into, device):
        cp = sems.copy(out, into, device)
        cp.start()
        stage[key] = cp

    def first(h):
        n = YFIRST[h]
        m = PANELS - n
        far_out, far_in = s[f"far_out{h}"], s[f"far_in{h}"]
        y1_out, y1_in = s[f"y1_out{h}"], s[f"y1_in{h}"]
        for dy in (2, 1, 3, 0):
            need(h, dy)
            if dy == 2:
                for side in range(2):
                    for i in range(n):
                        far_out[side, i] = both(h, 2, side, i).astype(BF16)
                    post(stage1, (h, "far", side), far_out.at[side], far_in.at[side], at_y(1 - 2 * side))
            elif dy:
                side = dy // 2
                dx = 1 - side
                for i in range(n):
                    y1_out[side, dx, i] = both(h, dy, dx, i).astype(BF16)
                post(stage1, (h, "y", side, dx), y1_out.at[side, dx], y1_in.at[side, dx], at_y(1 - 2 * side))
            for i in range(m):
                s[f"x1_out{h}"][dy, i] = both(h, dy, 1, n + i).astype(BF16)
            if m:
                post(stage1, (h, "x", dy), s[f"x1_out{h}"].at[dy], s[f"x1_in{h}"].at[dy], x_far)

    def middle(h):
        n = YFIRST[h]
        y1_out, y1_in = s[f"y1_out{h}"], s[f"y1_in{h}"]
        for side in range(2):
            stage1[h, "far", side].wait_recv()
            dy, dx = 1 + 2 * side, side
            for i in range(n):
                total = both(h, dy, dx, i) + s[f"far_in{h}"][side, i].astype(F32)
                y1_out[side, dx, i] = total.astype(BF16)
            post(stage1, (h, "y", side, dx), y1_out.at[side, dx], y1_in.at[side, dx], at_y(1 - 2 * side))

    def second(h):
        n = YFIRST[h]
        m = PANELS - n
        if m:
            for dy in (2, 1, 3):
                stage1[h, "x", dy].wait_recv()
                for i in range(m):
                    total = both(h, dy, 0, n + i) + s[f"x1_in{h}"][dy, i].astype(F32)
                    s[f"y2_out{h}"][dy - 1, i] = total.astype(BF16)
                post(stage2, (h, dy), s[f"y2_out{h}"].at[dy - 1], s[f"y2_in{h}"].at[dy - 1], at_y(dy))
        for side in range(2):
            stage1[h, "y", side, 1].wait_recv()
        for i in range(n):
            total = both(h, 0, 1, i)
            for side in range(2):
                total += s[f"y1_in{h}"][side, 1, i].astype(F32)
            s[f"x2_out{h}"][i] = total.astype(BF16)
        post(stage2, (h, "x"), s[f"x2_out{h}"], s[f"x2_in{h}"], x_far)

    def third(h):
        n = YFIRST[h]
        m = PANELS - n
        ends = [(stage1, (h, "x", 0))] + [(stage2, (h, dy)) for dy in (2, 1, 3)] if m else []
        for i in (*range(n, PANELS), *range(n)):
            if i == 0:
                ends = [(stage1, (h, "y", side, 0)) for side in range(2)] + [(stage2, (h, "x"))]
            for stage, key in ends:
                stage[key].wait_recv()
            ends = []
            total = both(h, 0, 0, i)
            if i < n:
                for side in range(2):
                    total += s[f"y1_in{h}"][side, 0, i].astype(F32)
                total += s[f"x2_in{h}"][i].astype(F32)
            else:
                total += s[f"x1_in{h}"][0, i - n].astype(F32)
                for dy in (2, 1, 3):
                    total += s[f"y2_in{h}"][dy - 1, i - n].astype(F32)
            mean = (total / s["deg"][i]).astype(BF16)
            mixed = s["mixed"][i] + jnp.dot(
                mean, s["wn"][h * TILE : (h + 1) * TILE, :], preferred_element_type=F32
            )
            if h < HALVES - 1:
                s["mixed"][i] = mixed
            else:
                s["hidden"][i] = jnp.maximum(mixed, 0.0).astype(BF16)
                cp = pltpu.make_async_copy(s["hidden"].at[i], out_ref.at[i], local.at[i])
                cp.start()
                hidden_copies.append(cp)

    products(0, 0, 48)
    arrive(1, 3, 0)
    arrive(1, 3, 1)
    cross(1, 3)
    gathered, sems.copies = sems.copies, []
    products(0, 48, 96)
    exchange(0)
    degree1()
    first(0)
    products(1, 0, 48)
    middle(0)
    products(1, 48, 96)
    exchange(1)
    degree2()
    first(1)
    for cp in gathered:
        cp.wait_send()
    degree3()
    middle(1)
    second(0)
    reducing, sems.copies = sems.copies, []
    second(1)
    third(0)
    for cp in reducing:
        cp.wait_send()
    third(1)
    for cp in hidden_copies:
        cp.wait()
    sems.sent()


def scratch_spec():
    panel = lambda *lead: pltpu.VMEM((*lead, TILE, TILE), BF16)
    spec = {
        "send_sem": pltpu.SemaphoreType.DMA((112,)),
        "recv_sem": pltpu.SemaphoreType.DMA((112,)),
        "local_sem": pltpu.SemaphoreType.DMA((HALVES + CHUNKS + 10,)),
        "own": panel(HALVES, PANELS),
        "lists_vec": pltpu.VMEM((CAP, ROWS), jnp.int32),
        "lists": pltpu.SMEM((CAP, ROWS), jnp.int32),
        "rows_vec": pltpu.VMEM((1, TILES), jnp.int32),
        "count": pltpu.SMEM((1, 1), jnp.int32),
        "cols": pltpu.SMEM((1, TILES), jnp.int32),
        "bias": pltpu.VMEM((1, 2 * TILE), F32),
        "ws": pltpu.VMEM((2 * TILE, 2 * TILE), BF16),
        "wn": pltpu.VMEM((2 * TILE, 2 * TILE), BF16),
        "tiles32": pltpu.VMEM((TILES, TILE, TILE), jnp.int32),
        "blocks": panel(TILES),
        "degs": pltpu.VMEM((TILE, TILE), F32),
        "deg0_out": pltpu.VMEM((2, 2, Y, 8, TILE), F32),
        "deg0_in": pltpu.VMEM((2, Y, 8, TILE), F32),
        "deg1_out": pltpu.VMEM((2, Y, 8, TILE), F32),
        "deg1_in": pltpu.VMEM((Y, 8, TILE), F32),
        "deg2_out": pltpu.VMEM((Y, 8, TILE), F32),
        "deg2_in": pltpu.VMEM((Y - 1, 8, TILE), F32),
        "deg": pltpu.VMEM((PANELS, TILE, TILE), F32),
        "rows": pltpu.VMEM((8, TILE), jnp.int32),
        "meta": pltpu.VMEM((8, TILE), jnp.int32),
        "meta_smem": pltpu.SMEM((8, TILE), jnp.int32),
        "lists_out": pltpu.VMEM((8, TILE), jnp.int32),
        "lists_in": pltpu.VMEM((8, TILE), jnp.int32),
        "lists_smem": pltpu.SMEM((8, TILE), jnp.int32),
        "hidden": pltpu.VMEM((PANELS, TILE, 2 * TILE), BF16),
        "mixed": pltpu.VMEM((PANELS, TILE, 2 * TILE), F32),
        "swap_out": panel(HALVES, 8 * PANELS),
        "swap_in": panel(HALVES, 8 * PANELS),
    }
    for h in range(HALVES):
        for k in range(3):
            spec[f"fwd{h}{k}"] = panel(PANELS)
            spec[f"bwd{h}{k}"] = panel(PANELS)
        spec[f"opp{h}"] = panel(PANELS)
        spec[f"oper{h}"] = panel(ROWS * CAP)
        spec[f"pair{h}"] = panel(8 * CAP)
        spec[f"sums{h}"] = pltpu.VMEM((TILES + 1, TILE, TILE), F32)
        n = YFIRST[h]
        m = PANELS - n
        for end in ("out", "in"):
            spec[f"far_{end}{h}"] = panel(2, n)
            spec[f"y1_{end}{h}"] = panel(2, 2, n)
            spec[f"x2_{end}{h}"] = panel(n)
        if m:
            spec[f"x1_out{h}"] = panel(4, m)
            spec[f"x1_in{h}"] = panel(4, m)
            spec[f"y2_out{h}"] = panel(3, m)
            spec[f"y2_in{h}"] = panel(3, m)
    return spec


SCRATCH_NAMES = list(scratch_spec())


def shards(
    features, tiles, tile_rows, tile_cols, tile_count, panel_lists, self_weight, neigh_weight, bias
):
    hbm = pl.BlockSpec(memory_space=pltpu.HBM)
    lists = panel_lists[0, 0].T
    hidden = pl.pallas_call(
        kernel,
        out_shape=jax.ShapeDtypeStruct((PANELS, TILE, 2 * TILE), BF16),
        in_specs=[hbm] * 9,
        out_specs=hbm,
        scratch_shapes=list(scratch_spec().values()),
        compiler_params=pltpu.CompilerParams(
            collective_id=0, has_side_effects=True, vmem_limit_bytes=56 << 20
        ),
        name="sage",
    )(
        features.reshape(PANELS, TILE, 2 * TILE),
        tiles[0, 0],
        tile_rows[0],
        tile_cols[0],
        tile_count,
        lists,
        self_weight,
        neigh_weight,
        bias.reshape(1, 2 * TILE),
    )
    return hidden.reshape(PANELS * TILE, 2 * TILE)


def solution(mesh):
    return jax.shard_map(
        shards,
        mesh=mesh,
        in_specs=(
            P(("row", "col"), None),
            P("row", "col", None, None, None),
            P("row", "col", None),
            P("row", "col", None),
            P("row", "col"),
            P("row", "col", None, None),
            P(),
            P(),
            P(),
        ),
        out_specs=P(("row", "col"), None),
        check_vma=False,
    )
```

```python
import functools

import jax
import jax.numpy as jnp
from jax import lax
from jax.experimental import pallas as pl
from jax.experimental.pallas import tpu as pltpu
from jax.sharding import PartitionSpec as P

MESH = pl.DeviceIdType.MESH
Z = 8
Y = 4
TILE = 128
HALVES = 2
PANELS = 4
TILES = 96
CAP = 2
COLS = 16
ROWS = 16
CHUNKS = 4
YFIRST = (2, 2)

F32 = jnp.float32
BF16 = jnp.bfloat16


class Sems:
    def __init__(self, send, recv):
        self.send, self.recv, self.used, self.copies = send, recv, 0, []

    def copy(self, src, dst, device):
        n = self.used
        self.used += 1
        c = pltpu.make_async_remote_copy(
            src_ref=src,
            dst_ref=dst,
            send_sem=self.send.at[n],
            recv_sem=self.recv.at[n],
            device_id=device,
            device_id_type=MESH,
        )
        self.copies.append(c)
        return c

    def sent(self):
        for c in self.copies:
            c.wait_send()
        self.copies = []


def kernel(
    feat_ref,
    tiles_ref,
    rows_hbm,
    cols_hbm,
    count_hbm,
    lists_hbm,
    ws_hbm,
    wn_hbm,
    bias_hbm,
    out_ref,
    *scratch,
):
    s = dict(zip(SCRATCH_NAMES, scratch))
    r, c = lax.axis_index("row"), lax.axis_index("col")
    x_lo, z = r // Z, lax.rem(r, Z)
    y, x_hi, core = c // 4, lax.rem(c // 2, 2), lax.rem(c, 2)

    def z_at(d):
        return lax.rem(z + d + Z, Z)

    def at_z(d):
        return (x_lo * Z + z_at(d), c)

    def at_y(d):
        return (r, lax.rem(c + 4 * d + COLS, COLS))

    x_pair = ((1 - x_lo) * Z + z, c)
    x_far = (r, c + 2 - 4 * x_hi)
    sibling = (r, c + 1 - 2 * core)

    barrier = pltpu.get_barrier_semaphore()
    peers = [at_z(1), at_z(-1), x_pair, sibling, x_far, at_y(1), at_y(2), at_y(3)]
    for peer in peers:
        pl.semaphore_signal(barrier, inc=1, device_id=peer, device_id_type=MESH)

    local = s["local_sem"]
    own_copies = []
    for h in range(HALVES):
        cp = pltpu.make_async_copy(
            feat_ref.at[:, :, pl.ds(h * TILE, TILE)], s["own"].at[h], local.at[h]
        )
        cp.start()
        own_copies.append(cp)
    small_copies, weight_copies = [], []
    for k, (src, dst) in enumerate(
        (
            (lists_hbm, s["lists_vec"]),
            (lists_hbm, s["lists"]),
            (rows_hbm, s["rows_vec"]),
            (count_hbm, s["count"]),
            (cols_hbm, s["cols"]),
            (bias_hbm, s["bias"]),
            (ws_hbm, s["ws"]),
            (wn_hbm, s["wn"]),
        )
    ):
        cp = pltpu.make_async_copy(src, dst, local.at[HALVES + CHUNKS + 2 + k])
        cp.start()
        (small_copies if k < 5 else weight_copies).append(cp)
    per = TILES // CHUNKS

    pl.semaphore_wait(barrier, len(peers))

    sems = Sems(s["send_sem"], s["recv_sem"])
    for cp in own_copies:
        cp.wait()

    fwd = [[s[f"fwd{h}{k}"] for k in range(3)] for h in range(HALVES)]
    bwd = [[s[f"bwd{h}{k}"] for k in range(3)] for h in range(HALVES)]
    opp = [s["opp0"], s["opp1"]]
    oper = [s["oper0"], s["oper1"]]
    ring = {}
    for h in range(HALVES):
        for k in range(4):
            for q in range(2):
                part = pl.ds(2 * q, 2)
                for way, chain in ((0, fwd[h]), (1, bwd[h])):
                    if k == 3 and q != way:
                        continue
                    src = s["own"].at[h] if k == 0 else chain[k - 1]
                    dst = chain[k] if k < 3 else opp[h]
                    ring[h, way, k, q] = sems.copy(
                        src.at[part], dst.at[part], at_z(1 - 2 * way)
                    )
    lists_copy = sems.copy(s["lists_out"], s["lists_in"], x_pair)

    for cp in small_copies:
        cp.wait()
    lists_ref, cols_ref = s["lists"], s["cols"]

    def send(h, q):
        for way in range(2):
            ring[h, way, 0, q].start()

    send(0, 0)
    send(0, 1)
    s["lists_out"][...] = jnp.zeros((8, TILE), jnp.int32)
    s["lists_out"][0:CAP, 0:ROWS] = s["lists_vec"][...]
    lists_copy.start()
    send(1, 0)
    send(1, 1)
    tile_copies = []
    for k in range(CHUNKS):
        part = pl.ds(k * per, per)
        cp = pltpu.make_async_copy(
            tiles_ref.at[part], s["tiles32"].at[part], local.at[HALVES + k]
        )
        cp.start()
        tile_copies.append(cp)

    pair_copies = {}

    def select(h, slot, block, dist):
        owner = x_lo * Z + z_at(dist)
        for j in range(CAP):
            mine = jnp.maximum(lists_ref[j, owner], 0)
            oper[h][owner * CAP + j] = block[mine]
        for j in range(CAP):
            theirs = jnp.maximum(s["lists_smem"][j, owner], 0)
            s[f"pair{h}"][slot * CAP + j] = block[theirs]
        cp = sems.copy(
            s[f"pair{h}"].at[pl.ds(slot * CAP, CAP)],
            oper[h].at[pl.ds(owner * CAP, CAP)],
            x_pair,
        )
        cp.start()
        pair_copies[h, slot] = cp

    live = s["count"][0, 0]
    lane = lax.broadcasted_iota(jnp.int32, (TILE, TILE), 1)
    sub = lax.broadcasted_iota(jnp.int32, (TILE, TILE), 0)
    s["rows"][...] = jnp.full((8, TILE), -1, jnp.int32)
    s["rows"][0:1, 0:TILES] = s["rows_vec"][...]
    row_l = jnp.broadcast_to(s["rows"][0:1, :], (TILE, TILE))
    row_l = jnp.where(lane < live, row_l, -1)
    row_s = jnp.transpose(row_l.astype(F32)).astype(jnp.int32)
    prev = jnp.max(jnp.where((row_s == row_l) & (sub < lane), sub, -1), axis=0, keepdims=True)
    prev = jnp.where(prev < 0, TILES, prev)
    last = jnp.max(jnp.where(row_s == lane, sub, -1), axis=0, keepdims=True)
    last = jnp.where(last < 0, TILES, last)
    s["meta"][0:1, :] = prev
    s["meta"][1:2, :] = last
    s["meta"][2:8, :] = jnp.zeros((6, TILE), jnp.int32)
    meta_copy = pltpu.make_async_copy(s["meta"], s["meta_smem"], local.at[HALVES + CHUNKS])
    meta_copy.start()

    for h in range(HALVES):
        s[f"sums{h}"][TILES] = jnp.zeros((TILE, TILE), F32)

    ones = jnp.ones((16, TILE), BF16)

    def prepare(lo, hi):
        for k in range(CHUNKS):
            if lo <= k * per < hi:
                tile_copies[k].wait()

        def body(t, _):
            block = s["tiles32"][t].astype(F32).astype(BF16)
            s["blocks"][t] = block
            sums = lax.dot_general(
                ones, block, (((1,), (1,)), ((), ())), preferred_element_type=F32
            )
            s["degs"][pl.ds(t, 1), :] = sums[0:1, :]
            return 0

        lax.fori_loop(lo, hi, body, 0, unroll=True)

    def arrive(h, k, q):
        for way in range(2):
            if (h, way, k, q) in ring:
                ring[h, way, k, q].wait_recv()
            if (h, way, k + 1, q) in ring:
                ring[h, way, k + 1, q].start()

    def cross(h, k):
        if k < 3:
            select(h, 1 + k, fwd[h][k], -(k + 1))
            select(h, 4 + k, bwd[h][k], k + 1)
        else:
            select(h, 7, opp[h], 4)

    def base(i):
        mixed = jnp.dot(s["own"][0, i], s["ws"][0:TILE, :], preferred_element_type=F32)
        mixed += jnp.dot(s["own"][1, i], s["ws"][TILE : 2 * TILE, :], preferred_element_type=F32)
        s["mixed"][i] = mixed + s["bias"][...]

    prepare(0, 12)
    lists_copy.wait_recv()
    smem_copy = pltpu.make_async_copy(
        s["lists_in"], s["lists_smem"], local.at[HALVES + CHUNKS + 1]
    )
    smem_copy.start()
    smem_copy.wait()
    for h in range(HALVES):
        select(h, 0, s["own"].at[h], 0)

    deg = {}

    def degree0():
        q = lax.broadcasted_iota(jnp.int32, (TILE, TILE), 0)
        b = q // 8
        owner = lax.rem(b, 4) * 4 + lax.rem(b // 4, 2) * 2 + b // 8
        panel = jnp.where(lax.rem(q, 8) < PANELS, owner * PANELS + lax.rem(q, 8), -2)
        hot = (panel == row_l).astype(F32).astype(BF16)
        s["degs"][TILES:TILE, :] = jnp.zeros((TILE - TILES, TILE), F32)
        degs = jnp.dot(hot, s["degs"][...].astype(BF16), preferred_element_type=F32)
        s["deg0_out"][...] = degs.reshape(2, 2, Y, 8, TILE)
        deg[0] = sems.copy(s["deg0_out"].at[1 - core], s["deg0_in"], sibling)
        deg[0].start()

    def degree1():
        deg[0].wait_recv()
        s["deg1_out"][...] = s["deg0_out"][core] + s["deg0_in"][...]
        deg[1] = sems.copy(s["deg1_out"].at[1 - x_hi], s["deg1_in"], x_far)
        deg[1].start()

    def degree2():
        deg[1].wait_recv()
        s["deg2_out"][...] = s["deg1_out"][x_hi] + s["deg1_in"][...]
        for dy in range(1, Y):
            to = lax.rem(y + dy, Y)
            deg[2, dy] = sems.copy(s["deg2_out"].at[to], s["deg2_in"].at[dy - 1], at_y(dy))
            deg[2, dy].start()

    def degree3():
        total = s["deg2_out"][y]
        for dy in range(1, Y):
            deg[2, dy].wait_recv()
            total += s["deg2_in"][dy - 1]
        total = jnp.maximum(total, 1.0)
        wide = jnp.transpose(jnp.concatenate([total] * 16, axis=0))
        for i in range(PANELS):
            s["deg"][i] = jnp.broadcast_to(wide[:, i : i + 1], (TILE, TILE))

    arrive(0, 0, 0)
    arrive(0, 0, 1)
    cross(0, 0)
    prepare(12, 36)
    arrive(1, 0, 0)
    arrive(1, 0, 1)
    cross(1, 0)
    prepare(36, 60)
    arrive(0, 1, 0)
    arrive(0, 1, 1)
    cross(0, 1)
    prepare(60, 84)
    arrive(1, 1, 0)
    arrive(1, 1, 1)
    cross(1, 1)
    prepare(84, 96)
    degree0()
    arrive(0, 2, 0)
    arrive(0, 2, 1)
    cross(0, 2)
    arrive(0, 3, 0)
    arrive(0, 3, 1)
    cross(0, 3)
    arrive(1, 2, 0)
    arrive(1, 2, 1)
    cross(1, 2)
    for cp in weight_copies:
        cp.wait()
    for i in range(PANELS):
        base(i)
    meta_copy.wait()

    def products(h, lo, hi):
        if lo == 0:
            for slot in range(8):
                pair_copies[h, slot].wait_recv()
        sums = s[f"sums{h}"]

        def body(t, _):
            value = jnp.dot(
                s["blocks"][t], oper[h][cols_ref[0, t]], preferred_element_type=F32
            )
            sums[t] = value + sums[s["meta_smem"][0, t]]
            return 0

        lax.fori_loop(lo, hi, body, 0, unroll=48)

    def owner_col(dy, dx, which):
        hi = x_hi if dx == 0 else 1 - x_hi
        return lax.rem(y + dy, Y) * 4 + hi * 2 + which

    order = [(2, 1), (2, 0), (1, 1), (1, 0), (3, 1), (3, 0), (0, 1), (0, 0)]
    swap = {}

    def partial(h, dy, dx, which, i):
        p = owner_col(dy, dx, which) * PANELS + i
        return s[f"sums{h}"][s["meta_smem"][1, p]]

    def exchange(h):
        for dy, dx in order:
            j = dy * 2 + dx

            def body(i, _):
                s["swap_out"][h, j * PANELS + i] = partial(h, dy, dx, 1 - core, i).astype(BF16)
                return 0

            lax.fori_loop(0, PANELS, body, 0, unroll=True)
            part = pl.ds(j * PANELS, PANELS)
            cp = sems.copy(s["swap_out"].at[h, part], s["swap_in"].at[h, part], sibling)
            cp.start()
            swap[h, j] = cp

    def both(h, dy, dx, i):
        j = dy * 2 + dx
        return partial(h, dy, dx, core, i) + s["swap_in"][h, j * PANELS + i].astype(F32)

    stage1, stage2, arrived, hidden_copies = {}, {}, set(), []

    def need(h, dy):
        for dx in (1, 0):
            if (h, dy, dx) not in arrived:
                arrived.add((h, dy, dx))
                swap[h, dy * 2 + dx].wait_recv()

    def post(stage, key, out, into, device):
        cp = sems.copy(out, into, device)
        cp.start()
        stage[key] = cp

    def first(h):
        n = YFIRST[h]
        m = PANELS - n
        far_out, far_in = s[f"far_out{h}"], s[f"far_in{h}"]
        y1_out, y1_in = s[f"y1_out{h}"], s[f"y1_in{h}"]
        for dy in (2, 1, 3, 0):
            need(h, dy)
            if dy == 2:
                for side in range(2):
                    for i in range(n):
                        far_out[side, i] = both(h, 2, side, i).astype(BF16)
                    post(stage1, (h, "far", side), far_out.at[side], far_in.at[side], at_y(1 - 2 * side))
            elif dy:
                side = dy // 2
                dx = 1 - side
                for i in range(n):
                    y1_out[side, dx, i] = both(h, dy, dx, i).astype(BF16)
                post(stage1, (h, "y", side, dx), y1_out.at[side, dx], y1_in.at[side, dx], at_y(1 - 2 * side))
            for i in range(m):
                s[f"x1_out{h}"][dy, i] = both(h, dy, 1, n + i).astype(BF16)
            if m:
                post(stage1, (h, "x", dy), s[f"x1_out{h}"].at[dy], s[f"x1_in{h}"].at[dy], x_far)

    def middle(h):
        n = YFIRST[h]
        y1_out, y1_in = s[f"y1_out{h}"], s[f"y1_in{h}"]
        for side in range(2):
            stage1[h, "far", side].wait_recv()
            dy, dx = 1 + 2 * side, side
            for i in range(n):
                total = both(h, dy, dx, i) + s[f"far_in{h}"][side, i].astype(F32)
                y1_out[side, dx, i] = total.astype(BF16)
            post(stage1, (h, "y", side, dx), y1_out.at[side, dx], y1_in.at[side, dx], at_y(1 - 2 * side))

    def second(h):
        n = YFIRST[h]
        m = PANELS - n
        if m:
            for dy in (2, 1, 3):
                stage1[h, "x", dy].wait_recv()
                for i in range(m):
                    total = both(h, dy, 0, n + i) + s[f"x1_in{h}"][dy, i].astype(F32)
                    s[f"y2_out{h}"][dy - 1, i] = total.astype(BF16)
                post(stage2, (h, dy), s[f"y2_out{h}"].at[dy - 1], s[f"y2_in{h}"].at[dy - 1], at_y(dy))
        for side in range(2):
            stage1[h, "y", side, 1].wait_recv()
        for i in range(n):
            total = both(h, 0, 1, i)
            for side in range(2):
                total += s[f"y1_in{h}"][side, 1, i].astype(F32)
            s[f"x2_out{h}"][i] = total.astype(BF16)
        post(stage2, (h, "x"), s[f"x2_out{h}"], s[f"x2_in{h}"], x_far)

    def third(h):
        n = YFIRST[h]
        m = PANELS - n
        ends = [(stage1, (h, "x", 0))] + [(stage2, (h, dy)) for dy in (2, 1, 3)] if m else []
        for i in (*range(n, PANELS), *range(n)):
            if i == 0:
                ends = [(stage1, (h, "y", side, 0)) for side in range(2)] + [(stage2, (h, "x"))]
            for stage, key in ends:
                stage[key].wait_recv()
            ends = []
            total = both(h, 0, 0, i)
            if i < n:
                for side in range(2):
                    total += s[f"y1_in{h}"][side, 0, i].astype(F32)
                total += s[f"x2_in{h}"][i].astype(F32)
            else:
                total += s[f"x1_in{h}"][0, i - n].astype(F32)
                for dy in (2, 1, 3):
                    total += s[f"y2_in{h}"][dy - 1, i - n].astype(F32)
            mean = (total / s["deg"][i]).astype(BF16)
            mixed = s["mixed"][i] + jnp.dot(
                mean, s["wn"][h * TILE : (h + 1) * TILE, :], preferred_element_type=F32
            )
            if h < HALVES - 1:
                s["mixed"][i] = mixed
            else:
                s["hidden"][i] = jnp.maximum(mixed, 0.0).astype(BF16)
                cp = pltpu.make_async_copy(s["hidden"].at[i], out_ref.at[i], local.at[i])
                cp.start()
                hidden_copies.append(cp)

    products(0, 0, 48)
    arrive(1, 3, 0)
    arrive(1, 3, 1)
    cross(1, 3)
    gathered, sems.copies = sems.copies, []
    products(0, 48, 96)
    exchange(0)
    degree1()
    first(0)
    products(1, 0, 48)
    middle(0)
    products(1, 48, 96)
    exchange(1)
    degree2()
    first(1)
    for cp in gathered:
        cp.wait_send()
    degree3()
    middle(1)
    second(0)
    reducing, sems.copies = sems.copies, []
    second(1)
    third(0)
    for cp in reducing:
        cp.wait_send()
    third(1)
    for cp in hidden_copies:
        cp.wait()
    sems.sent()


def scratch_spec():
    panel = lambda *lead: pltpu.VMEM((*lead, TILE, TILE), BF16)
    spec = {
        "send_sem": pltpu.SemaphoreType.DMA((112,)),
        "recv_sem": pltpu.SemaphoreType.DMA((112,)),
        "local_sem": pltpu.SemaphoreType.DMA((HALVES + CHUNKS + 10,)),
        "own": panel(HALVES, PANELS),
        "lists_vec": pltpu.VMEM((CAP, ROWS), jnp.int32),
        "lists": pltpu.SMEM((CAP, ROWS), jnp.int32),
        "rows_vec": pltpu.VMEM((1, TILES), jnp.int32),
        "count": pltpu.SMEM((1, 1), jnp.int32),
        "cols": pltpu.SMEM((1, TILES), jnp.int32),
        "bias": pltpu.VMEM((1, 2 * TILE), F32),
        "ws": pltpu.VMEM((2 * TILE, 2 * TILE), BF16),
        "wn": pltpu.VMEM((2 * TILE, 2 * TILE), BF16),
        "tiles32": pltpu.VMEM((TILES, TILE, TILE), jnp.int32),
        "blocks": panel(TILES),
        "degs": pltpu.VMEM((TILE, TILE), F32),
        "deg0_out": pltpu.VMEM((2, 2, Y, 8, TILE), F32),
        "deg0_in": pltpu.VMEM((2, Y, 8, TILE), F32),
        "deg1_out": pltpu.VMEM((2, Y, 8, TILE), F32),
        "deg1_in": pltpu.VMEM((Y, 8, TILE), F32),
        "deg2_out": pltpu.VMEM((Y, 8, TILE), F32),
        "deg2_in": pltpu.VMEM((Y - 1, 8, TILE), F32),
        "deg": pltpu.VMEM((PANELS, TILE, TILE), F32),
        "rows": pltpu.VMEM((8, TILE), jnp.int32),
        "meta": pltpu.VMEM((8, TILE), jnp.int32),
        "meta_smem": pltpu.SMEM((8, TILE), jnp.int32),
        "lists_out": pltpu.VMEM((8, TILE), jnp.int32),
        "lists_in": pltpu.VMEM((8, TILE), jnp.int32),
        "lists_smem": pltpu.SMEM((8, TILE), jnp.int32),
        "hidden": pltpu.VMEM((PANELS, TILE, 2 * TILE), BF16),
        "mixed": pltpu.VMEM((PANELS, TILE, 2 * TILE), F32),
        "swap_out": panel(HALVES, 8 * PANELS),
        "swap_in": panel(HALVES, 8 * PANELS),
    }
    for h in range(HALVES):
        for k in range(3):
            spec[f"fwd{h}{k}"] = panel(PANELS)
            spec[f"bwd{h}{k}"] = panel(PANELS)
        spec[f"opp{h}"] = panel(PANELS)
        spec[f"oper{h}"] = panel(ROWS * CAP)
        spec[f"pair{h}"] = panel(8 * CAP)
        spec[f"sums{h}"] = pltpu.VMEM((TILES + 1, TILE, TILE), F32)
        n = YFIRST[h]
        m = PANELS - n
        for end in ("out", "in"):
            spec[f"far_{end}{h}"] = panel(2, n)
            spec[f"y1_{end}{h}"] = panel(2, 2, n)
            spec[f"x2_{end}{h}"] = panel(n)
        if m:
            spec[f"x1_out{h}"] = panel(4, m)
            spec[f"x1_in{h}"] = panel(4, m)
            spec[f"y2_out{h}"] = panel(3, m)
            spec[f"y2_in{h}"] = panel(3, m)
    return spec


SCRATCH_NAMES = list(scratch_spec())


def shards(
    features, tiles, tile_rows, tile_cols, tile_count, panel_lists, self_weight, neigh_weight, bias
):
    hbm = pl.BlockSpec(memory_space=pltpu.HBM)
    lists = panel_lists[0, 0].T
    hidden = pl.pallas_call(
        kernel,
        out_shape=jax.ShapeDtypeStruct((PANELS, TILE, 2 * TILE), BF16),
        in_specs=[hbm] * 9,
        out_specs=hbm,
        scratch_shapes=list(scratch_spec().values()),
        compiler_params=pltpu.CompilerParams(
            collective_id=0, has_side_effects=True, vmem_limit_bytes=56 << 20
        ),
        name="sage",
    )(
        features.reshape(PANELS, TILE, 2 * TILE),
        tiles[0, 0],
        tile_rows[0],
        tile_cols[0],
        tile_count,
        lists,
        self_weight,
        neigh_weight,
        bias.reshape(1, 2 * TILE),
    )
    return hidden.reshape(PANELS * TILE, 2 * TILE)


def solution(mesh):
    return jax.shard_map(
        shards,
        mesh=mesh,
        in_specs=(
            P(("row", "col"), None),
            P("row", "col", None, None, None),
            P("row", "col", None),
            P("row", "col", None),
            P("row", "col"),
            P("row", "col", None, None),
            P(),
            P(),
            P(),
        ),
        out_specs=P(("row", "col"), None),
        check_vma=False,
    )
```
